256 devices in a mesh: slab: 32 (over y, x, core), coil: 8 (over z).
Axes of the slice: x: 4, y: 4, z: 8, core: 2. Of those that a mesh axis runs over, the one named last changes fastest.
Arguments:
- image_est: bfloat16 [2, 256, 256, 256], P(None, 'slab', 'coil'), may hold values from -6 to 6
- coil_maps: bfloat16 [8, 2, 256, 256, 256], P('coil', None, 'slab'), may hold values from -6 to 6
- kernel_tiles: bfloat16 [5120, 128, 256], P('slab'), may hold values from -0.375 to 0.375
- tile_ids: int32 [5120], P('slab'), may hold values from 0 to 2047, as said below
- tile_count: int32 [32], P('slab'), may hold values from 1 to 160, as said below
- measured: float32 [8, 2, 5120, 128], P('coil', None, 'slab'), may hold values from -6 to 6
Outputs:
- residual: float32 [8, 2, 5120, 128], P('coil', None, 'slab')
- rms: float32 [1], replicated
The draws below stay inside these ranges and needn't reach their ends.
Inputs may be any that keep to these rules, and one draw needn't show every extreme that they name: The live slots of a slab are its first tile_count slots; some slab has all 160 live. `tile_ids`: the slots of one slab read distinct tiles.
All inputs are finite; a program needn't handle non-finite values.
Results may differ from the reference program's by a relative error of at most 0.0003.
Values may be sent and summed in bfloat16 or wider, within the bound.
A program may use at most 192 MiB of HBM per device.

```python
import math
import jax
import jax.numpy as jnp
from jax import lax

IMG = 256
KXW = 64
MAXT = 160
TS = 128
TC = 256
SLABS = 32
COILS = 8
SLOTS = 5120
TILES_DEV = 2048
N_SLAB = 32


def draw_tile_count(key, part):
    key = jax.random.fold_in(key, 3)
    slab_index = jnp.arange(SLABS, dtype=jnp.int32)
    spread = jnp.abs(2 * slab_index - (SLABS - 1))
    jitter = jax.random.randint(key, (SLABS,), 0, MAXT // 4 + 1)
    counts = MAXT - MAXT // 2 * spread // SLABS - jitter
    chosen = jax.random.randint(jax.random.fold_in(key, 7), (), 0, SLABS)
    counts = jnp.where(slab_index == chosen, MAXT, counts)
    return jnp.clip(counts, 1, MAXT).astype(jnp.int32)


def draw_tile_ids(key, part):
    slab_keys = jax.random.split(jax.random.fold_in(key, 11), SLABS)
    marked = jax.random.randint(jax.random.fold_in(key, 13), (), 0, SLABS)
    value_index = jnp.arange(TILES_DEV, dtype=jnp.int32)

    def one_slab(slab_key, slab_number):
        perm = jax.random.permutation(slab_key, TILES_DEV).astype(jnp.int32)
        position = jnp.argsort(perm, stable=True).astype(jnp.int32)
        forced = jnp.where(value_index == 0, -2, jnp.where(value_index == TILES_DEV - 1, -1, position))
        score = jnp.where(slab_number == marked, forced, position)
        order = jnp.argsort(score, stable=True).astype(jnp.int32)
        return order[:MAXT]
    slab_numbers = jnp.arange(SLABS, dtype=jnp.int32)
    return jax.vmap(one_slab)(slab_keys, slab_numbers).reshape(SLABS * MAXT).astype(jnp.int32)


def block_scale(own_key, extent, pieces, low, top_value):
    loudness, own = 1.0, jax.random.fold_in(own_key, 6)
    for dim, shards_of in pieces:
        draws = jnp.exp(jax.random.uniform(jax.random.fold_in(own, dim), (shards_of,), jnp.float32, low / len(pieces), top_value / len(pieces)))
        loudness = loudness * jnp.repeat(draws, extent[dim] // shards_of).reshape([-1 if axis == dim else 1 for axis in range(len(extent))])
    return loudness


def centred(own_key, dims, scale, bound, cuts=(), held_as=jnp.bfloat16):
    result = jax.random.normal(own_key, dims, jnp.float32) * scale
    if len(cuts) > 0:
        result = block_scale(own_key, dims, cuts, -0.22, 0.18) * result
    return jnp.clip(result, min=-bound, max=bound).astype(held_as)


def setup_inputs(seed: int = 0) -> dict:
    key_list = jax.random.split(jax.random.key(seed), 7)
    image_est = centred(key_list[0], (2, IMG, IMG, IMG), 1.0, 6.0, ((1, 32), (2, 8)))
    coil_maps = centred(key_list[1], (COILS, 2, IMG, IMG, IMG), 1.0, 6.0, ((0, 8), (2, 32)))
    kernel_tiles = centred(key_list[2], (SLOTS, TS, TC), TC ** -0.5, 0.375, ((0, 32),))
    tile_ids = draw_tile_ids(jax.random.fold_in(key_list[6], 71), 0)
    tile_count = draw_tile_count(jax.random.fold_in(key_list[6], 71), 0)
    measured = centred(key_list[5], (COILS, 2, SLOTS, TS), 1.0, 6.0, ((0, 8), (2, 32)), jnp.float32)
    return {"image_est": image_est, "coil_maps": coil_maps, "kernel_tiles": kernel_tiles, "tile_ids": tile_ids, "tile_count": tile_count, "measured": measured}


def phase_table(row_count, col_count, row_offset, col_offset, modulus):
    row_index = jnp.arange(row_count, dtype=jnp.int32)[:, None] - row_offset
    col_index = jnp.arange(col_count, dtype=jnp.int32)[None, :] - col_offset
    phases = row_index * col_index % modulus
    angles = phases.astype(jnp.float32) * (2.0 * math.pi / modulus)
    return (jnp.cos(angles), jnp.sin(angles))

def rotate(real_part, imag_part, cosine, sine_table, form):
    precise = lax.Precision.HIGHEST
    out_real = jnp.einsum(form, real_part, cosine, precision=precise) + jnp.einsum(form, imag_part, sine_table, precision=precise)
    out_imag = jnp.einsum(form, imag_part, cosine, precision=precise) - jnp.einsum(form, real_part, sine_table, precision=precise)
    return (out_real, out_imag)

def reference(image_est, coil_maps, kernel_tiles, tile_ids, tile_count, measured):
    precise = lax.Precision.HIGHEST
    image_real = image_est[0].astype(jnp.float32)
    image_imag = image_est[1].astype(jnp.float32)
    slot_total = tile_ids.shape[0]
    per_slab = slot_total // N_SLAB
    slot_index = jnp.arange(slot_total, dtype=jnp.int32)
    slab_of = slot_index // per_slab
    live = slot_index % per_slab < tile_count[slab_of]
    kernel_float = kernel_tiles.astype(jnp.float32)
    x_cos, x_sin = phase_table(IMG, KXW, IMG // 2, KXW // 2, 2 * IMG)
    z_cos, z_sin = phase_table(IMG, 2 * IMG, 0, 0, 2 * IMG)
    y_cos, y_sin = phase_table(IMG, 2 * IMG, IMG // 2, IMG, 2 * IMG)
    scale = float(IMG) ** (-1.5)

    def one_coil(inputs):
        maps, observed = inputs
        map_real = maps[0].astype(jnp.float32)
        map_imag = maps[1].astype(jnp.float32)
        weight_real = image_real * map_real - image_imag * map_imag
        weight_imag = image_real * map_imag + image_imag * map_real
        x_real, x_imag = rotate(weight_real, weight_imag, x_cos, x_sin, 'zyx,xj->zjy')
        z_real, z_imag = rotate(x_real, x_imag, z_cos, z_sin, 'zjy,zk->kjy')
        g_real, g_imag = rotate(z_real, z_imag, y_cos, y_sin, 'kjy,ym->kjm')
        grid = jnp.stack([g_real, g_imag]) * scale
        tiles = grid.reshape(2, N_SLAB, 2 * IMG // N_SLAB // 4, 4, KXW // 8, 8, 2 * IMG // 8, 8)
        tiles = tiles.transpose(1, 2, 4, 6, 0, 3, 5, 7).reshape(N_SLAB, -1, 2, 256)
        cells = tiles[slab_of, tile_ids]
        predicted = jnp.einsum('sic,src->rsi', kernel_float, cells, precision=precise)
        return jnp.where(live[None, :, None], predicted - observed, 0.0)
    residual = lax.map(one_coil, (coil_maps, measured))
    rms = jnp.sqrt(jnp.sum(residual * residual) / residual.size).reshape(1)
    return (residual, rms)
```

```python
import jax
import jax.numpy as jnp
import ml_dtypes
import numpy as np
from jax import lax
from jax.experimental import pallas as pl
from jax.experimental.pallas import tpu as pltpu
from jax.sharding import PartitionSpec as P

F32 = jnp.float32
BF16 = jnp.bfloat16
MESH = pl.DeviceIdType.MESH

IMG = 256
KXW = 64
FREQ = 512
SLABS = 32
COILS = 8
PLANES = 8
YB = 32
LANES = 128
KZ = 16
SLOTS = 160
CHUNKS = ((0,), (1, 7), (2, 6), (3, 5), (4,))


def split_table(table):
    table = table.astype(np.float32)
    high = table.astype(ml_dtypes.bfloat16)
    low = (table - high.astype(np.float32)).astype(ml_dtypes.bfloat16)
    return high, low


def angles(rows, cols, row_offset, col_offset):
    index = (np.arange(rows)[:, None] - row_offset) * (np.arange(cols)[None, :] - col_offset)
    return (index % FREQ) * (2.0 * np.pi / FREQ)


def x_table():
    phase = angles(IMG, KXW, IMG // 2, KXW // 2)
    cosine, sine = np.cos(phase) / 4096.0, np.sin(phase) / 4096.0
    table = np.block([[cosine, -sine], [sine, cosine]])
    high, low = split_table(table)
    return np.concatenate([high, low], axis=1)


def long_table(row_offset, col_offset):
    phase = angles(FREQ, IMG, row_offset, col_offset)
    high, low = split_table(np.concatenate([np.cos(phase), np.sin(phase)], axis=1))
    return np.concatenate([high, high, low], axis=1)


def place_table():
    table = np.zeros((8, 2, 64, 2, 256), np.float32)
    for w in range(8):
        for part in range(2):
            for u in range(4):
                for v in range(8):
                    table[w, part, 8 * u + v, part, 64 * u + 8 * v + w] = 1.0
    return table.reshape(1024, 512).astype(ml_dtypes.bfloat16)


def split(value):
    high = value.astype(BF16)
    low = (value - high.astype(F32)).astype(BF16)
    return high, low


def kernel(
    img_hbm, maps_hbm, kern_hbm, ids, count, meas, tx_hbm, ez_hbm, ey_hbm, place_hbm,
    res, rms,
    img, maps, kern, tx, ez, ey, place,
    send_a, lines, send_b, planes, grid, picked, cells, sums_c, sums_s,
    load_sem, ring_send, ring_recv, a_send, a_recv, b_send, b_recv, sum_send, sum_recv,
):
    me = lax.axis_index("slab")
    coil = lax.axis_index("coil")
    left = lax.rem(coil + COILS - 1, COILS)
    right = lax.rem(coil + 1, COILS)

    def load(index, src, dst):
        copy = pltpu.make_async_copy(src, dst, load_sem.at[index])
        copy.start()
        return copy

    load_img = load(0, img_hbm, img.at[0])
    load_maps = load(1, maps_hbm.at[0], maps)
    load_tx = load(2, tx_hbm, tx)
    load_ez = load(3, ez_hbm, ez)
    load_ey = load(4, ey_hbm, ey)
    load_place = load(5, place_hbm, place)
    load_kern = load(6, kern_hbm, kern)

    barrier = pltpu.get_barrier_semaphore()

    @pl.loop(1, SLABS)
    def _(step):
        pl.semaphore_signal(
            barrier, inc=1, device_id={"slab": lax.rem(me + step, SLABS)}, device_id_type=MESH
        )

    @pl.loop(1, COILS)
    def _(step):
        pl.semaphore_signal(
            barrier, inc=1, device_id={"coil": lax.rem(coil + step, COILS)}, device_id_type=MESH
        )

    pl.semaphore_wait(barrier, SLABS - 1 + COILS - 1)

    def hop(direction, step, part):
        target = left if direction == 0 else right
        dst_slot = step if direction == 0 else 8 - step
        src_slot = (dst_slot - 1) if direction == 0 else (dst_slot + 1) % 8
        src = img_hbm.at[part] if step == 1 else img.at[src_slot, part]
        return pltpu.make_async_remote_copy(
            src_ref=src,
            dst_ref=img.at[dst_slot, part],
            send_sem=ring_send.at[direction, step - 1, part],
            recv_sem=ring_recv.at[direction, step - 1, part],
            device_id={"coil": target},
            device_id_type=MESH,
        )

    hops = {}
    for direction in range(2):
        for step in range(1, 5):
            for part in range(2):
                if step < 4 or part == direction:
                    hops[direction, step, part] = hop(direction, step, part)

    for part in range(2):
        for direction in range(2):
            hops[direction, 1, part].start()

    def arrive(step):
        for part in range(2):
            for direction in range(2):
                if (direction, step, part) in hops:
                    hops[direction, step, part].wait_recv()
                    if (direction, step + 1, part) in hops:
                        hops[direction, step + 1, part].start()

    lane = lax.broadcasted_iota(jnp.int32, (1, LANES), 1)
    sign = jnp.where(lane < 64, 1.0, -1.0).astype(F32)

    def along_x(slot, entry):
        block = lax.rem(coil + slot, COILS)
        rows = pl.ds(pl.multiple_of(block * YB, YB), YB)
        ar = img[slot, 0].astype(F32)
        ai = img[slot, 1].astype(F32)
        sr = maps[0, :, rows, :].astype(F32)
        si = maps[1, :, rows, :].astype(F32)
        wr = (ar * sr - ai * si).reshape(PLANES * YB, IMG)
        wi = (ar * si + ai * sr).reshape(PLANES * YB, IMG)
        high, low = split(jnp.concatenate([wr, wi], axis=1))
        both = jnp.dot(high, tx[...], preferred_element_type=F32)
        out = both[:, :LANES] + both[:, LANES:]
        out = out + jnp.dot(low, tx[:, :LANES], preferred_element_type=F32)
        for z in range(PLANES):
            send_a[entry, pl.ds(z, YB, stride=PLANES), :] = out[z * YB : (z + 1) * YB]

    def exchange(src, dst, chunk, width, send_sem, recv_sem):
        entries = pl.ds(2 * chunk, len(CHUNKS[chunk]))
        mine = pl.ds(pl.multiple_of(me * width, width), width)

        @pl.loop(1, SLABS)
        def _(step):
            peer = lax.rem(me + step, SLABS)
            theirs = pl.ds(pl.multiple_of(peer * width, width), width)
            pltpu.make_async_remote_copy(
                src_ref=src.at[entries, theirs],
                dst_ref=dst.at[entries, mine],
                send_sem=send_sem.at[chunk],
                recv_sem=recv_sem.at[chunk],
                device_id={"slab": peer},
                device_id_type=MESH,
            ).start()

        dst[entries, mine, :] = src[entries, mine, :]

    def wait_all(ref, chunk, width, sem):
        part = ref.at[pl.ds(2 * chunk, len(CHUNKS[chunk])), pl.ds(0, (SLABS - 1) * width)]
        pltpu.make_async_copy(part, part, sem.at[chunk]).wait()

    def turned(value):
        swapped = [
            sign * pltpu.roll(value[:, i : i + LANES], 64, 1) for i in range(0, value.shape[1], LANES)
        ]
        return jnp.concatenate([value, jnp.concatenate(swapped, axis=1)], axis=0)

    def transform(table, value):
        high, low = split(turned(value))
        return jnp.dot(
            table[...], jnp.concatenate([high, low, high], axis=0), preferred_element_type=F32
        )

    def stage_x(chunk):
        for i, slot in enumerate(CHUNKS[chunk]):
            along_x(slot, 2 * chunk + i)
        exchange(send_a, lines, chunk, PLANES, a_send, a_recv)

    def stage_z(chunk):
        wait_all(lines, chunk, PLANES, a_recv)
        count_here = len(CHUNKS[chunk])
        value = jnp.concatenate([lines[2 * chunk + i] for i in range(count_here)], axis=1)
        out = transform(ez, value)
        for i in range(count_here):
            send_b[2 * chunk + i] = out[:, i * LANES : (i + 1) * LANES]
        exchange(send_b, planes, chunk, KZ, b_send, b_recv)

    load_img.wait()
    load_maps.wait()
    load_tx.wait()
    stage_x(0)
    load_ez.wait()
    for chunk in range(1, 5):
        arrive(chunk)
        stage_x(chunk)
        stage_z(chunk - 1)
    stage_z(4)
    load_ey.wait()
    load_place.wait()
    load_kern.wait()
    for chunk in range(5):
        wait_all(planes, chunk, KZ, b_recv)

    def entry_of(block):
        slot = lax.rem(block - coil + COILS, COILS)
        return jnp.where(slot <= 4, 2 * slot, 2 * (COILS - slot) + 1)

    entries = [entry_of(block) for block in range(COILS)]

    @pl.loop(0, KZ // 2)
    def _(pair):
        halves = []
        for odd in range(2):
            halves.append(
                jnp.concatenate(
                    [planes[e, pl.ds(2 * pair + odd, SLABS, stride=KZ), :] for e in entries], axis=0
                )
            )
        out = transform(ey, jnp.concatenate(halves, axis=1))
        for odd in range(2):
            half = out[:, odd * LANES : (odd + 1) * LANES].reshape(64, 8, LANES)
            grid[pl.ds((2 * pair + odd) * 64, 64)] = half

    place_of = lax.broadcasted_iota(jnp.int32, (8, LANES), 1) // 8

    @pl.loop(0, SLOTS, unroll=4)
    def _(slot):
        tile = ids[slot]
        first = (tile >> 9) * 256 + (tile & 63)
        b = jnp.full((8, LANES), (tile >> 6) & 7, jnp.int32)
        away = (place_of - b) & 7
        total = jnp.zeros((8, LANES), F32)
        for u in range(4):
            value = grid[first + 64 * u]
            total = jnp.where(away == u, pltpu.roll(value, 8 * u, 1) if u else value, total)
        for bit in (1, 2, 4):
            total = jnp.where((b & bit) > 0, pltpu.roll(total, LANES - 8 * bit, 1), total)
        picked[pl.ds(pl.multiple_of(slot * 8, 8), 8), :] = total

    high_sum = jnp.zeros((SLOTS, 512), F32)
    low_sum = jnp.zeros((SLOTS, 512), F32)
    for w in range(8):
        high, low = split(picked[pl.ds(w, SLOTS, stride=8), :])
        spot = place[w * LANES : (w + 1) * LANES, :]
        high_sum = high_sum + jnp.dot(high, spot, preferred_element_type=F32)
        low_sum = low_sum + jnp.dot(low, spot, preferred_element_type=F32)
    cells[0] = high_sum
    cells[1] = low_sum

    live = count[0]
    row = lax.broadcasted_iota(jnp.int32, (8, LANES), 0)
    row4 = lax.rem(lax.broadcasted_iota(jnp.int32, (32, LANES), 0), 8)

    def degrid(index, squares):
        first = pl.multiple_of(index * 8, 8)
        rows = pl.ds(first, 8)
        left_side = jnp.concatenate(
            [
                cells[0, rows, :256], cells[1, rows, :256],
                cells[0, rows, 256:], cells[1, rows, 256:],
            ],
            axis=0,
        ).astype(BF16)
        total = jnp.zeros((32, LANES), F32)
        for s in range(8):
            product = lax.dot_general(
                left_side, kern[first + s], (((1,), (1,)), ((), ())), preferred_element_type=F32
            )
            total = jnp.where(row4 == s, product, total)
        alive = first + row < live
        for part in range(2):
            predicted = total[16 * part : 16 * part + 8] + total[16 * part + 8 : 16 * part + 16]
            value = jnp.where(alive, predicted - meas[0, part, rows, :], 0.0)
            res[0, part, rows, :] = value
            squares = squares + value * value
        return squares

    squares = lax.fori_loop(0, SLOTS // 8, degrid, jnp.zeros((8, LANES), F32))

    def total_over(buffer, axis, position, size, which, value):
        buffer[position] = value

        @pl.loop(1, size)
        def _(step):
            pltpu.make_async_remote_copy(
                src_ref=buffer.at[position],
                dst_ref=buffer.at[position],
                send_sem=sum_send.at[which],
                recv_sem=sum_recv.at[which],
                device_id={axis: lax.rem(position + step, size)},
                device_id_type=MESH,
            ).start()

        others = buffer.at[pl.ds(0, size - 1)]
        pltpu.make_async_copy(others, others, sum_recv.at[which]).wait()
        return jnp.sum(buffer[...], axis=0)

    squares = total_over(sums_c, "coil", coil, COILS, 0, squares)
    squares = total_over(sums_s, "slab", me, SLABS, 1, squares)
    total = jnp.sum(jnp.sum(squares, axis=1, keepdims=True), axis=0, keepdims=True)
    root = jnp.sqrt(total * (1.0 / (COILS * 2 * SLABS * SLOTS * LANES)))
    rms[...] = jnp.broadcast_to(root, (8, LANES))

    for copy in hops.values():
        copy.wait_send()
    for chunk in range(5):
        wait_all(send_a, chunk, PLANES, a_send)
        wait_all(send_b, chunk, KZ, b_send)
    for which, (buffer, size) in enumerate(((sums_c, COILS), (sums_s, SLABS))):
        others = buffer.at[pl.ds(0, size - 1)]
        pltpu.make_async_copy(others, others, sum_send.at[which]).wait()


def per_device(image_est, coil_maps, kernel_tiles, tile_ids, tile_count, measured):
    hbm = pl.BlockSpec(memory_space=pl.ANY)
    vmem = pl.BlockSpec(memory_space=pltpu.VMEM)
    smem = pl.BlockSpec(memory_space=pltpu.SMEM)
    tables = [
        jnp.asarray(x_table()),
        jnp.asarray(long_table(0, 0)),
        jnp.asarray(long_table(FREQ // 2, IMG // 2)),
        jnp.asarray(place_table()),
    ]
    residual, rms = pl.pallas_call(
        kernel,
        out_shape=(
            jax.ShapeDtypeStruct((1, 2, SLOTS, LANES), F32),
            jax.ShapeDtypeStruct((8, LANES), F32),
        ),
        in_specs=[hbm, hbm, hbm, smem, smem, vmem, hbm, hbm, hbm, hbm],
        out_specs=(vmem, vmem),
        scratch_shapes=[
            pltpu.VMEM((8, 2, PLANES, YB, IMG), BF16),
            pltpu.VMEM((2, PLANES, IMG, IMG), BF16),
            pltpu.VMEM((SLOTS, LANES, 256), BF16),
            pltpu.VMEM((2 * IMG, 2 * LANES), BF16),
            pltpu.VMEM((FREQ, 6 * IMG), BF16),
            pltpu.VMEM((FREQ, 6 * IMG), BF16),
            pltpu.VMEM((1024, 512), BF16),
            pltpu.VMEM((10, SLABS * PLANES, LANES), F32),
            pltpu.VMEM((10, SLABS * PLANES, LANES), F32),
            pltpu.VMEM((10, FREQ, LANES), F32),
            pltpu.VMEM((10, FREQ, LANES), F32),
            pltpu.VMEM((KZ * 64, 8, LANES), F32),
            pltpu.VMEM((SLOTS * 8, LANES), F32),
            pltpu.VMEM((2, SLOTS, 512), F32),
            pltpu.VMEM((COILS, 8, LANES), F32),
            pltpu.VMEM((SLABS, 8, LANES), F32),
            pltpu.SemaphoreType.DMA((7,)),
            pltpu.SemaphoreType.DMA((2, 4, 2)),
            pltpu.SemaphoreType.DMA((2, 4, 2)),
            pltpu.SemaphoreType.DMA((5,)),
            pltpu.SemaphoreType.DMA((5,)),
            pltpu.SemaphoreType.DMA((5,)),
            pltpu.SemaphoreType.DMA((5,)),
            pltpu.SemaphoreType.DMA((2,)),
            pltpu.SemaphoreType.DMA((2,)),
        ],
        compiler_params=pltpu.CompilerParams(
            collective_id=0, has_side_effects=True, vmem_limit_bytes=56 * 1024 * 1024
        ),
        cost_estimate=pl.CostEstimate(
            flops=6_000_000_000, bytes_accessed=20_000_000, transcendentals=0
        ),
    )(image_est, coil_maps, kernel_tiles, tile_ids, tile_count, measured, *tables)
    return residual, rms[0, :1]


def solution(mesh):
    placed = (
        P(None, "slab", "coil", None),
        P("coil", None, "slab", None, None),
        P("slab", None, None),
        P("slab"),
        P("slab"),
        P("coil", None, "slab", None),
    )
    return jax.shard_map(
        per_device,
        mesh=mesh,
        in_specs=placed,
        out_specs=(P("coil", None, "slab", None), P()),
        check_vma=False,
    )
```

```python
import jax
import jax.numpy as jnp
import ml_dtypes
import numpy as np
from jax import lax
from jax.experimental import pallas as pl
from jax.experimental.pallas import tpu as pltpu
from jax.sharding import PartitionSpec as P

F32 = jnp.float32
BF16 = jnp.bfloat16
MESH = pl.DeviceIdType.MESH

IMG = 256
KXW = 64
FREQ = 512
SLABS = 32
COILS = 8
PLANES = 8
YB = 32
LANES = 128
KZ = 16
SLOTS = 160
STEPS = 32760.0
CHUNKS = ((0,), (1, 7), (2, 6), (3, 5), (4,))


def split_table(table):
    table = table.astype(np.float32)
    high = table.astype(ml_dtypes.bfloat16)
    low = (table - high.astype(np.float32)).astype(ml_dtypes.bfloat16)
    return high, low


def angles(rows, cols, row_offset, col_offset):
    index = (np.arange(rows)[:, None] - row_offset) * (np.arange(cols)[None, :] - col_offset)
    return (index % FREQ) * (2.0 * np.pi / FREQ)


def x_table():
    phase = angles(IMG, KXW, IMG // 2, KXW // 2)
    cosine, sine = np.cos(phase) / 4096.0, np.sin(phase) / 4096.0
    table = np.block([[cosine, -sine], [sine, cosine]])
    high, low = split_table(table)
    return np.concatenate([high, low], axis=1)


def long_table(row_offset, col_offset):
    phase = angles(FREQ, IMG, row_offset, col_offset)
    high, low = split_table(np.concatenate([np.cos(phase), np.sin(phase)], axis=1))
    return np.concatenate([high, high, low], axis=1)


def place_table():
    table = np.zeros((8, 2, 64, 2, 256), np.float32)
    for w in range(8):
        for part in range(2):
            for u in range(4):
                for v in range(8):
                    table[w, part, 8 * u + v, part, 64 * u + 8 * v + w] = 1.0
    return table.reshape(1024, 512).astype(ml_dtypes.bfloat16)


def split(value):
    high = value.astype(BF16)
    low = (value - high.astype(F32)).astype(BF16)
    return high, low


def kernel(
    img_hbm, maps_hbm, kern_hbm, ids_hbm, count_hbm, meas_hbm, tx_hbm, ez_hbm, ey_hbm, place_hbm,
    res, rms,
    img, maps, kern, ids, count, meas, tx, ez, ey, place,
    send_a, lines, send_b, planes, send_q, coded, send_s, scales, grid, picked, cells,
    sums_c, sums_s,
    load_sem, ring_send, ring_recv, a_send, a_recv, b_send, b_recv, s_send, s_recv,
    sum_send, sum_recv,
):
    me = lax.axis_index("slab")
    coil = lax.axis_index("coil")
    left = lax.rem(coil + COILS - 1, COILS)
    right = lax.rem(coil + 1, COILS)

    def load(index, src, dst):
        copy = pltpu.make_async_copy(src, dst, load_sem.at[index])
        copy.start()
        return copy

    barrier = pltpu.get_barrier_semaphore()

    @pl.loop(1, SLABS)
    def _(step):
        pl.semaphore_signal(
            barrier, inc=1, device_id={"slab": lax.rem(me + step, SLABS)}, device_id_type=MESH
        )

    @pl.loop(1, COILS)
    def _(step):
        pl.semaphore_signal(
            barrier, inc=1, device_id={"coil": lax.rem(coil + step, COILS)}, device_id_type=MESH
        )

    load_img = load(0, img_hbm, img.at[0])
    load_maps = load(1, maps_hbm.at[0], maps)
    load_tx = load(2, tx_hbm, tx)
    pl.semaphore_wait(barrier, SLABS - 1 + COILS - 1)

    def hop(direction, step, part):
        target = left if direction == 0 else right
        dst_slot = step if direction == 0 else 8 - step
        src_slot = (dst_slot - 1) if direction == 0 else (dst_slot + 1) % 8
        src = img_hbm.at[part] if step == 1 else img.at[src_slot, part]
        return pltpu.make_async_remote_copy(
            src_ref=src,
            dst_ref=img.at[dst_slot, part],
            send_sem=ring_send.at[direction, step - 1, part],
            recv_sem=ring_recv.at[direction, step - 1, part],
            device_id={"coil": target},
            device_id_type=MESH,
        )

    hops = {}
    for direction in range(2):
        for step in range(1, 5):
            for part in range(2):
                if step < 4 or part == direction:
                    hops[direction, step, part] = hop(direction, step, part)

    for part in range(2):
        for direction in range(2):
            hops[direction, 1, part].start()

    load_ez = load(3, ez_hbm, ez)
    late_loads = [
        load(4, ey_hbm, ey),
        load(5, place_hbm, place),
        load(6, kern_hbm, kern),
        load(7, ids_hbm, ids),
        load(8, count_hbm, count),
        load(9, meas_hbm.at[0], meas),
    ]

    def arrive(step):
        for part in range(2):
            for direction in range(2):
                if (direction, step, part) in hops:
                    hops[direction, step, part].wait_recv()
                    if (direction, step + 1, part) in hops:
                        hops[direction, step + 1, part].start()

    lane = lax.broadcasted_iota(jnp.int32, (1, LANES), 1)
    sign = jnp.where(lane < 64, 1.0, -1.0).astype(F32)

    def along_x(slot, entry):
        block = lax.rem(coil + slot, COILS)
        rows = pl.ds(pl.multiple_of(block * YB, YB), YB)
        ar = img[slot, 0].astype(F32)
        ai = img[slot, 1].astype(F32)
        sr = maps[0, :, rows, :].astype(F32)
        si = maps[1, :, rows, :].astype(F32)
        wr = (ar * sr - ai * si).reshape(PLANES * YB, IMG)
        wi = (ar * si + ai * sr).reshape(PLANES * YB, IMG)
        high, low = split(jnp.concatenate([wr, wi], axis=1))
        both = jnp.dot(high, tx[...], preferred_element_type=F32)
        out = both[:, :LANES] + both[:, LANES:]
        out = out + jnp.dot(low, tx[:, :LANES], preferred_element_type=F32)
        for z in range(PLANES):
            send_a[entry, pl.ds(z, YB, stride=PLANES), :] = out[z * YB : (z + 1) * YB]

    def exchange(src, dst, first, number, width, send_sem, recv_sem):
        entries = pl.ds(first, number)
        mine = pl.ds(pl.multiple_of(me * width, width), width)

        @pl.loop(1, SLABS)
        def _(step):
            peer = lax.rem(me + step, SLABS)
            theirs = pl.ds(pl.multiple_of(peer * width, width), width)
            pltpu.make_async_remote_copy(
                src_ref=src.at[entries, theirs],
                dst_ref=dst.at[entries, mine],
                send_sem=send_sem,
                recv_sem=recv_sem,
                device_id={"slab": peer},
                device_id_type=MESH,
            ).start()

        dst[entries, mine, :] = src[entries, mine, :]

    def wait_all(ref, number, width, sem):
        part = ref.at[pl.ds(0, number), pl.ds(0, (SLABS - 1) * width)]
        pltpu.make_async_copy(part, part, sem).wait()

    def turned(value):
        swapped = [
            sign * pltpu.roll(value[:, i : i + LANES], 64, 1) for i in range(0, value.shape[1], LANES)
        ]
        return jnp.concatenate([value, jnp.concatenate(swapped, axis=1)], axis=0)

    def transform(table, value):
        high, low = split(turned(value))
        return jnp.dot(
            table[...], jnp.concatenate([high, low, high], axis=0), preferred_element_type=F32
        )

    def stage_x(chunk):
        for i, slot in enumerate(CHUNKS[chunk]):
            along_x(slot, 2 * chunk + i)
        number = len(CHUNKS[chunk])
        exchange(
            send_a, lines, 2 * chunk, number, PLANES, a_send.at[chunk], a_recv.at[chunk]
        )

    def stage_z(chunk):
        number = len(CHUNKS[chunk])
        first = 2 * chunk
        wait_all(lines, number, PLANES, a_recv.at[chunk])
        value = jnp.concatenate([lines[first + i] for i in range(number)], axis=1)
        out = transform(ez, value)
        for i in range(number):
            send_b[first + i] = out[:, i * LANES : (i + 1) * LANES]
        if chunk == 4:
            exchange(
                send_b, planes, first, number, KZ, b_send.at[chunk], b_recv.at[chunk]
            )
            return

        @pl.loop(0, SLABS, unroll=4)
        def _(owner):
            rows = pl.ds(pl.multiple_of(owner * KZ, KZ), KZ)
            for i in range(number):
                block = send_b[first + i, rows, :]
                top = jnp.maximum(jnp.max(jnp.abs(block), axis=0, keepdims=True), 1e-30)
                send_q[first + i, rows, :] = jnp.round(block * (STEPS / top)).astype(jnp.int16)
                send_s[0, pl.ds(owner * 8 + first + i, 1), :] = top * (1.0 / STEPS)

        exchange(send_q, coded, first, number, KZ, b_send.at[chunk], b_recv.at[chunk])
        if chunk == 3:
            exchange(send_s, scales, 0, 1, 8, s_send.at[0], s_recv.at[0])

    send_s[...] = jnp.zeros((1, SLABS * 8, LANES), F32)
    load_img.wait()
    load_maps.wait()
    load_tx.wait()
    stage_x(0)
    load_ez.wait()
    for chunk in range(1, 5):
        arrive(chunk)
        stage_x(chunk)
        stage_z(chunk - 1)
    stage_z(4)
    for copy in late_loads:
        copy.wait()
    wait_all(scales, 1, 8, s_recv.at[0])
    for chunk in range(4):
        wait_all(coded, len(CHUNKS[chunk]), KZ, b_recv.at[chunk])

    @pl.loop(0, SLABS, unroll=2)
    def _(source):
        rows = pl.ds(pl.multiple_of(source * KZ, KZ), KZ)
        for entry in (0, 2, 3, 4, 5, 6, 7):
            scale = scales[0, pl.ds(source * 8 + entry, 1), :]
            planes[entry, rows, :] = coded[entry, rows, :].astype(F32) * scale

    wait_all(planes, 1, KZ, b_recv.at[4])

    def entry_of(block):
        slot = lax.rem(block - coil + COILS, COILS)
        return jnp.where(slot <= 4, 2 * slot, 2 * (COILS - slot) + 1)

    entries = [entry_of(block) for block in range(COILS)]

    @pl.loop(0, KZ // 2)
    def _(pair):
        halves = []
        for odd in range(2):
            halves.append(
                jnp.concatenate(
                    [planes[e, pl.ds(2 * pair + odd, SLABS, stride=KZ), :] for e in entries], axis=0
                )
            )
        out = transform(ey, jnp.concatenate(halves, axis=1))
        for odd in range(2):
            half = out[:, odd * LANES : (odd + 1) * LANES].reshape(64, 8, LANES)
            grid[pl.ds((2 * pair + odd) * 64, 64)] = half

    place_of = lax.broadcasted_iota(jnp.int32, (8, LANES), 1) // 8

    @pl.loop(0, SLOTS // 8)
    def _(index):
        found = []
        for k in range(8):
            tile = ids[index * 8 + k]
            first = (tile >> 9) * 256 + (tile & 63)
            b = jnp.full((8, LANES), (tile >> 6) & 7, jnp.int32)
            away = (place_of - b) & 7
            total = jnp.zeros((8, LANES), F32)
            for u in range(4):
                value = grid[first + 64 * u]
                total = jnp.where(away == u, pltpu.roll(value, 8 * u, 1) if u else value, total)
            for bit in (1, 2, 4):
                total = jnp.where((b & bit) > 0, pltpu.roll(total, LANES - 8 * bit, 1), total)
            found.append(total)
        picked[pl.ds(pl.multiple_of(index * 64, 64), 64), :] = jnp.concatenate(found, axis=0)

    high_sum = jnp.zeros((SLOTS, 512), F32)
    low_sum = jnp.zeros((SLOTS, 512), F32)
    for w in range(8):
        high, low = split(picked[pl.ds(w, SLOTS, stride=8), :])
        spot = place[w * LANES : (w + 1) * LANES, :]
        high_sum = high_sum + jnp.dot(high, spot, preferred_element_type=F32)
        low_sum = low_sum + jnp.dot(low, spot, preferred_element_type=F32)
    cells[0] = high_sum
    cells[1] = low_sum

    live = count[0]
    row = lax.broadcasted_iota(jnp.int32, (8, LANES), 0)
    row4 = lax.rem(lax.broadcasted_iota(jnp.int32, (32, LANES), 0), 8)

    def degrid(index, squares):
        first = pl.multiple_of(index * 8, 8)
        rows = pl.ds(first, 8)
        left_side = jnp.concatenate(
            [
                cells[0, rows, :256], cells[1, rows, :256],
                cells[0, rows, 256:], cells[1, rows, 256:],
            ],
            axis=0,
        ).astype(BF16)
        total = jnp.zeros((32, LANES), F32)
        for s in range(8):
            product = lax.dot_general(
                left_side, kern[first + s], (((1,), (1,)), ((), ())), preferred_element_type=F32
            )
            total = jnp.where(row4 == s, product, total)
        alive = first + row < live
        for part in range(2):
            predicted = total[16 * part : 16 * part + 8] + total[16 * part + 8 : 16 * part + 16]
            value = jnp.where(alive, predicted - meas[part, rows, :], 0.0)
            res[0, part, rows, :] = value
            squares = squares + value * value
        return squares

    squares = lax.fori_loop(0, SLOTS // 8, degrid, jnp.zeros((8, LANES), F32))

    def total_over(buffer, axis, position, size, which, value):
        buffer[position] = value

        @pl.loop(1, size)
        def _(step):
            pltpu.make_async_remote_copy(
                src_ref=buffer.at[position],
                dst_ref=buffer.at[position],
                send_sem=sum_send.at[which],
                recv_sem=sum_recv.at[which],
                device_id={axis: lax.rem(position + step, size)},
                device_id_type=MESH,
            ).start()

        others = buffer.at[pl.ds(0, size - 1)]
        pltpu.make_async_copy(others, others, sum_recv.at[which]).wait()
        return jnp.sum(buffer[...], axis=0)

    squares = total_over(sums_c, "coil", coil, COILS, 0, squares)
    squares = total_over(sums_s, "slab", me, SLABS, 1, squares)
    total = jnp.sum(jnp.sum(squares, axis=1, keepdims=True), axis=0, keepdims=True)
    root = jnp.sqrt(total * (1.0 / (COILS * 2 * SLABS * SLOTS * LANES)))
    rms[0] = root[0, 0]

    for copy in hops.values():
        copy.wait_send()
    for chunk in range(5):
        number = len(CHUNKS[chunk])
        wait_all(send_a, number, PLANES, a_send.at[chunk])
        wait_all(send_q if chunk < 4 else send_b, number, KZ, b_send.at[chunk])
    wait_all(send_s, 1, 8, s_send.at[0])
    for which, (buffer, size) in enumerate(((sums_c, COILS), (sums_s, SLABS))):
        others = buffer.at[pl.ds(0, size - 1)]
        pltpu.make_async_copy(others, others, sum_send.at[which]).wait()


def per_device(image_est, coil_maps, kernel_tiles, tile_ids, tile_count, measured):
    hbm = pl.BlockSpec(memory_space=pl.ANY)
    vmem = pl.BlockSpec(memory_space=pltpu.VMEM)
    smem = pl.BlockSpec(memory_space=pltpu.SMEM)
    tables = [
        jnp.asarray(x_table()),
        jnp.asarray(long_table(0, 0)),
        jnp.asarray(long_table(FREQ // 2, IMG // 2)),
        jnp.asarray(place_table()),
    ]
    residual, rms = pl.pallas_call(
        kernel,
        out_shape=(
            jax.ShapeDtypeStruct((1, 2, SLOTS, LANES), F32),
            jax.ShapeDtypeStruct((1,), F32),
        ),
        in_specs=[hbm] * 10,
        out_specs=(vmem, smem),
        scratch_shapes=[
            pltpu.VMEM((8, 2, PLANES, YB, IMG), BF16),
            pltpu.VMEM((2, PLANES, IMG, IMG), BF16),
            pltpu.VMEM((SLOTS, LANES, 256), BF16),
            pltpu.SMEM((SLOTS,), jnp.int32),
            pltpu.SMEM((1,), jnp.int32),
            pltpu.VMEM((2, SLOTS, LANES), F32),
            pltpu.VMEM((2 * IMG, 2 * LANES), BF16),
            pltpu.VMEM((FREQ, 6 * IMG), BF16),
            pltpu.VMEM((FREQ, 6 * IMG), BF16),
            pltpu.VMEM((1024, 512), BF16),
            pltpu.VMEM((10, SLABS * PLANES, LANES), F32),
            pltpu.VMEM((10, SLABS * PLANES, LANES), F32),
            pltpu.VMEM((10, FREQ, LANES), F32),
            pltpu.VMEM((10, FREQ, LANES), F32),
            pltpu.VMEM((8, FREQ, LANES), jnp.int16),
            pltpu.VMEM((8, FREQ, LANES), jnp.int16),
            pltpu.VMEM((1, SLABS * 8, LANES), F32),
            pltpu.VMEM((1, SLABS * 8, LANES), F32),
            pltpu.VMEM((KZ * 64, 8, LANES), F32),
            pltpu.VMEM((SLOTS * 8, LANES), F32),
            pltpu.VMEM((2, SLOTS, 512), F32),
            pltpu.VMEM((COILS, 8, LANES), F32),
            pltpu.VMEM((SLABS, 8, LANES), F32),
            pltpu.SemaphoreType.DMA((10,)),
            pltpu.SemaphoreType.DMA((2, 4, 2)),
            pltpu.SemaphoreType.DMA((2, 4, 2)),
            pltpu.SemaphoreType.DMA((5,)),
            pltpu.SemaphoreType.DMA((5,)),
            pltpu.SemaphoreType.DMA((5,)),
            pltpu.SemaphoreType.DMA((5,)),
            pltpu.SemaphoreType.DMA((1,)),
            pltpu.SemaphoreType.DMA((1,)),
            pltpu.SemaphoreType.DMA((2,)),
            pltpu.SemaphoreType.DMA((2,)),
        ],
        compiler_params=pltpu.CompilerParams(
            collective_id=0, has_side_effects=True, vmem_limit_bytes=56 * 1024 * 1024
        ),
        cost_estimate=pl.CostEstimate(
            flops=6_000_000_000, bytes_accessed=20_000_000, transcendentals=0
        ),
    )(image_est, coil_maps, kernel_tiles, tile_ids, tile_count, measured, *tables)
    return residual, rms


def solution(mesh):
    placed = (
        P(None, "slab", "coil", None),
        P("coil", None, "slab", None, None),
        P("slab", None, None),
        P("slab"),
        P("slab"),
        P("coil", None, "slab", None),
    )
    return jax.shard_map(
        per_device,
        mesh=mesh,
        in_specs=placed,
        out_specs=(P("coil", None, "slab", None), P()),
        check_vma=False,
    )
```

```python
import jax
import jax.numpy as jnp
import ml_dtypes
import numpy as np
from jax import lax
from jax.experimental import pallas as pl
from jax.experimental.pallas import tpu as pltpu
from jax.sharding import PartitionSpec as P

F32 = jnp.float32
BF16 = jnp.bfloat16
MESH = pl.DeviceIdType.MESH

IMG = 256
KXW = 64
FREQ = 512
SLABS = 32
COILS = 8
PLANES = 8
YB = 32
LANES = 128
KZ = 16
SLOTS = 160
STEPS = 32760.0
CHUNKS = ((0,), (1, 7), (2, 6), (3, 5), (4,))
FIRST = (0, 1, 3, 5, 7)
GROUPS = ((0, 1), (1, 3), (3, 5), (5, 9))
EXPONENTS = 8
FINE = 16.0


def split_table(table):
    table = table.astype(np.float32)
    high = table.astype(ml_dtypes.bfloat16)
    low = (table - high.astype(np.float32)).astype(ml_dtypes.bfloat16)
    return high, low


def angles(rows, cols, row_offset, col_offset):
    index = (np.arange(rows)[:, None] - row_offset) * (np.arange(cols)[None, :] - col_offset)
    return (index % FREQ) * (2.0 * np.pi / FREQ)


def x_table():
    phase = angles(IMG, KXW, IMG // 2, KXW // 2)
    cosine, sine = np.cos(phase) / 4096.0, np.sin(phase) / 4096.0
    table = np.block([[cosine, -sine], [sine, cosine]])
    high, low = split_table(table)
    return np.concatenate([high, low], axis=1)


def long_table(row_offset, col_offset):
    phase = angles(FREQ, IMG, row_offset, col_offset)
    high, low = split_table(np.concatenate([np.cos(phase), np.sin(phase)], axis=1))
    return np.concatenate([high, high, low], axis=1)


def place_table():
    table = np.zeros((8, 2, 64, 2, 256), np.float32)
    for w in range(8):
        for part in range(2):
            for u in range(4):
                for v in range(8):
                    table[w, part, 8 * u + v, part, 64 * u + 8 * v + w] = 1.0
    return table.reshape(1024, 512).astype(ml_dtypes.bfloat16)


def split(value):
    high = value.astype(BF16)
    low = (value - high.astype(F32)).astype(BF16)
    return high, low


def kernel(
    img_hbm, maps_hbm, kern_hbm, ids_hbm, count_hbm, meas_hbm, tx_hbm, ez_hbm, ey_hbm, place_hbm,
    res, rms,
    img, maps, kern, ids, count, meas, tx, ez, ey, place,
    send_a, lines, send_b, planes, send_q, coded, power, grid, picked, cells,
    sums_c, sums_s,
    load_sem, ring_send, ring_recv, a_send, a_recv, b_send, b_recv, sum_send, sum_recv,
):
    me = lax.axis_index("slab")
    coil = lax.axis_index("coil")
    left = lax.rem(coil + COILS - 1, COILS)
    right = lax.rem(coil + 1, COILS)

    def load(index, src, dst):
        copy = pltpu.make_async_copy(src, dst, load_sem.at[index])
        copy.start()
        return copy

    barrier = pltpu.get_barrier_semaphore()

    @pl.loop(1, SLABS)
    def _(step):
        pl.semaphore_signal(
            barrier, inc=1, device_id={"slab": lax.rem(me + step, SLABS)}, device_id_type=MESH
        )

    @pl.loop(1, COILS)
    def _(step):
        pl.semaphore_signal(
            barrier, inc=1, device_id={"coil": lax.rem(coil + step, COILS)}, device_id_type=MESH
        )

    load_img = load(0, img_hbm, img.at[0])
    load_maps = load(1, maps_hbm.at[0], maps)
    load_tx = load(2, tx_hbm, tx)
    pl.semaphore_wait(barrier, SLABS - 1 + COILS - 1)

    def hop(direction, step, part):
        target = left if direction == 0 else right
        dst_slot = step if direction == 0 else 8 - step
        src_slot = (dst_slot - 1) if direction == 0 else (dst_slot + 1) % 8
        src = img_hbm.at[part] if step == 1 else img.at[src_slot, part]
        return pltpu.make_async_remote_copy(
            src_ref=src,
            dst_ref=img.at[dst_slot, part],
            send_sem=ring_send.at[direction, step - 1, part],
            recv_sem=ring_recv.at[direction, step - 1, part],
            device_id={"coil": target},
            device_id_type=MESH,
        )

    hops = {}
    for direction in range(2):
        for step in range(1, 5):
            for part in range(2):
                if step < 4 or part == direction:
                    hops[direction, step, part] = hop(direction, step, part)

    for part in range(2):
        for direction in range(2):
            hops[direction, 1, part].start()

    load_ez = load(3, ez_hbm, ez)
    late_loads = [
        load(4, ey_hbm, ey),
        load(5, place_hbm, place),
        load(6, kern_hbm, kern),
        load(7, ids_hbm, ids),
        load(8, count_hbm, count),
        load(9, meas_hbm.at[0], meas),
    ]

    def arrive(step):
        for part in range(2):
            for direction in range(2):
                if (direction, step, part) in hops:
                    hops[direction, step, part].wait_recv()
                    if (direction, step + 1, part) in hops:
                        hops[direction, step + 1, part].start()

    lane = lax.broadcasted_iota(jnp.int32, (1, LANES), 1)
    sign = jnp.where(lane < 64, 1.0, -1.0).astype(F32)

    def along_x(slot, entry):
        block = lax.rem(coil + slot, COILS)
        rows = pl.ds(pl.multiple_of(block * YB, YB), YB)
        ar = img[slot, 0].astype(F32)
        ai = img[slot, 1].astype(F32)
        sr = maps[0, :, rows, :].astype(F32)
        si = maps[1, :, rows, :].astype(F32)
        wr = (ar * sr - ai * si).reshape(PLANES * YB, IMG)
        wi = (ar * si + ai * sr).reshape(PLANES * YB, IMG)
        high, low = split(jnp.concatenate([wr, wi], axis=1))
        both = jnp.dot(high, tx[...], preferred_element_type=F32)
        out = both[:, :LANES] + both[:, LANES:]
        out = out + jnp.dot(low, tx[:, :LANES], preferred_element_type=F32)
        for z in range(PLANES):
            send_a[entry, pl.ds(z, YB, stride=PLANES), :] = out[z * YB : (z + 1) * YB]

    def exchange(src, dst, first, number, width, send_sem, recv_sem):
        entries = pl.ds(first, number)
        mine = pl.ds(pl.multiple_of(me * width, width), width)

        @pl.loop(1, SLABS)
        def _(step):
            peer = lax.rem(me + step, SLABS)
            theirs = pl.ds(pl.multiple_of(peer * width, width), width)
            pltpu.make_async_remote_copy(
                src_ref=src.at[entries, theirs],
                dst_ref=dst.at[entries, mine],
                send_sem=send_sem,
                recv_sem=recv_sem,
                device_id={"slab": peer},
                device_id_type=MESH,
            ).start()

        dst[entries, mine, :] = src[entries, mine, :]

    def wait_all(ref, number, width, sem):
        part = ref.at[pl.ds(0, number), pl.ds(0, (SLABS - 1) * width)]
        pltpu.make_async_copy(part, part, sem).wait()

    def turned(value):
        swapped = [
            sign * pltpu.roll(value[:, i : i + LANES], 64, 1) for i in range(0, value.shape[1], LANES)
        ]
        return jnp.concatenate([value, jnp.concatenate(swapped, axis=1)], axis=0)

    def transform(table, value):
        high, low = split(turned(value))
        return jnp.dot(
            table[...], jnp.concatenate([high, low, high], axis=0), preferred_element_type=F32
        )

    def stage_x(chunk):
        for i, slot in enumerate(CHUNKS[chunk]):
            along_x(slot, FIRST[chunk] + i)
        number = len(CHUNKS[chunk])
        exchange(
            send_a, lines, FIRST[chunk], number, PLANES, a_send.at[chunk], a_recv.at[chunk]
        )

    def stage_z(chunk):
        number = len(CHUNKS[chunk])
        first = FIRST[chunk]
        wait_all(lines, number, PLANES, a_recv.at[chunk])
        value = jnp.concatenate([lines[first + i] for i in range(number)], axis=1)
        out = transform(ez, value)
        for i in range(number):
            send_b[first + i] = out[:, i * LANES : (i + 1) * LANES]

        @pl.loop(0, SLABS, unroll=4)
        def _(owner):
            rows = pl.ds(pl.multiple_of(owner * KZ, KZ), KZ)
            for i in range(number):
                block = send_b[first + i, rows, :]
                top = jnp.maximum(jnp.max(jnp.abs(block), axis=0, keepdims=True), 1e-30)
                exponent = jnp.ceil(jnp.log2(top) * FINE)
                factor = jnp.exp2(exponent * (-1.0 / FINE)) * STEPS
                send_q[first + i, rows, :] = jnp.round(block * factor).astype(jnp.int16)
                power[pl.ds(owner * KZ + first + i, 1), :] = exponent

    def stage_send(group):
        start, stop = GROUPS[group]
        if group == 3:
            send_q[EXPONENTS] = power[...].astype(jnp.int16)
        exchange(send_q, coded, start, stop - start, KZ, b_send.at[group], b_recv.at[group])

    power[...] = jnp.zeros((FREQ, LANES), F32)
    load_img.wait()
    load_maps.wait()
    load_tx.wait()
    stage_x(0)
    load_ez.wait()
    for chunk in range(1, 4):
        arrive(chunk)
        stage_x(chunk)
        stage_z(chunk - 1)
        stage_send(chunk - 1)
    arrive(4)
    stage_x(4)
    stage_z(3)
    stage_z(4)
    stage_send(3)
    for copy in late_loads:
        copy.wait()
    for group, (start, stop) in enumerate(GROUPS):
        wait_all(coded, stop - start, KZ, b_recv.at[group])
    power[...] = jnp.exp2(coded[EXPONENTS].astype(F32) * (1.0 / FINE)) * (1.0 / STEPS)

    @pl.loop(0, SLABS, unroll=4)
    def _(source):
        rows = pl.ds(pl.multiple_of(source * KZ, KZ), KZ)
        for entry in range(8):
            scale = power[pl.ds(source * KZ + entry, 1), :]
            planes[entry, rows, :] = coded[entry, rows, :].astype(F32) * scale

    def entry_of(block):
        slot = lax.rem(block - coil + COILS, COILS)
        return jnp.where(slot <= 4, jnp.maximum(2 * slot - 1, 0), 2 * (COILS - slot))

    entries = [entry_of(block) for block in range(COILS)]

    @pl.loop(0, KZ // 2)
    def _(pair):
        halves = []
        for odd in range(2):
            halves.append(
                jnp.concatenate(
                    [planes[e, pl.ds(2 * pair + odd, SLABS, stride=KZ), :] for e in entries], axis=0
                )
            )
        out = transform(ey, jnp.concatenate(halves, axis=1))
        for odd in range(2):
            half = out[:, odd * LANES : (odd + 1) * LANES].reshape(64, 8, LANES)
            grid[pl.ds((2 * pair + odd) * 64, 64)] = half

    place_of = lax.broadcasted_iota(jnp.int32, (8, LANES), 1) // 8

    @pl.loop(0, SLOTS // 32)
    def _(index):
        found = []
        for k in range(32):
            tile = ids[index * 32 + k]
            first = (tile >> 9) * 256 + (tile & 63)
            b = jnp.full((8, LANES), (tile >> 6) & 7, jnp.int32)
            away = (place_of - b) & 7
            total = jnp.zeros((8, LANES), F32)
            for u in range(4):
                value = grid[first + 64 * u]
                total = jnp.where(away == u, pltpu.roll(value, 8 * u, 1) if u else value, total)
            for bit in (1, 2, 4):
                total = jnp.where((b & bit) > 0, pltpu.roll(total, LANES - 8 * bit, 1), total)
            found.append(total)
        picked[pl.ds(pl.multiple_of(index * 256, 256), 256), :] = jnp.concatenate(found, axis=0)

    high_sum = jnp.zeros((SLOTS, 512), F32)
    low_sum = jnp.zeros((SLOTS, 512), F32)
    for w in range(8):
        high, low = split(picked[pl.ds(w, SLOTS, stride=8), :])
        spot = place[w * LANES : (w + 1) * LANES, :]
        high_sum = high_sum + jnp.dot(high, spot, preferred_element_type=F32)
        low_sum = low_sum + jnp.dot(low, spot, preferred_element_type=F32)
    cells[0] = high_sum
    cells[1] = low_sum

    live = count[0]
    row = lax.broadcasted_iota(jnp.int32, (8, LANES), 0)
    row4 = lax.rem(lax.broadcasted_iota(jnp.int32, (32, LANES), 0), 8)

    def degrid(index, squares):
        first = pl.multiple_of(index * 8, 8)
        rows = pl.ds(first, 8)
        left_side = jnp.concatenate(
            [
                cells[0, rows, :256], cells[1, rows, :256],
                cells[0, rows, 256:], cells[1, rows, 256:],
            ],
            axis=0,
        ).astype(BF16)
        total = jnp.zeros((32, LANES), F32)
        for s in range(0, 8, 2):
            product = lax.dot_general(
                left_side,
                kern[pl.ds(first + s, 2)].reshape(2 * LANES, 256),
                (((1,), (1,)), ((), ())),
                preferred_element_type=F32,
            )
            total = jnp.where(row4 == s, product[:, :LANES], total)
            total = jnp.where(row4 == s + 1, product[:, LANES:], total)
        alive = first + row < live
        for part in range(2):
            predicted = total[16 * part : 16 * part + 8] + total[16 * part + 8 : 16 * part + 16]
            value = jnp.where(alive, predicted - meas[part, rows, :], 0.0)
            res[0, part, rows, :] = value
            squares = squares + value * value
        return squares

    squares = lax.fori_loop(0, SLOTS // 8, degrid, jnp.zeros((8, LANES), F32))

    def total_over(buffer, axis, position, size, which, value):
        buffer[position] = value

        @pl.loop(1, size)
        def _(step):
            pltpu.make_async_remote_copy(
                src_ref=buffer.at[position],
                dst_ref=buffer.at[position],
                send_sem=sum_send.at[which],
                recv_sem=sum_recv.at[which],
                device_id={axis: lax.rem(position + step, size)},
                device_id_type=MESH,
            ).start()

        others = buffer.at[pl.ds(0, size - 1)]
        pltpu.make_async_copy(others, others, sum_recv.at[which]).wait()
        return jnp.sum(buffer[...], axis=0)

    squares = total_over(sums_c, "coil", coil, COILS, 0, squares)
    squares = total_over(sums_s, "slab", me, SLABS, 1, squares)
    total = jnp.sum(jnp.sum(squares, axis=1, keepdims=True), axis=0, keepdims=True)
    root = jnp.sqrt(total * (1.0 / (COILS * 2 * SLABS * SLOTS * LANES)))
    rms[0] = root[0, 0]

    for copy in hops.values():
        copy.wait_send()
    for chunk in range(5):
        wait_all(send_a, len(CHUNKS[chunk]), PLANES, a_send.at[chunk])
    for group, (start, stop) in enumerate(GROUPS):
        wait_all(send_q, stop - start, KZ, b_send.at[group])
    for which, (buffer, size) in enumerate(((sums_c, COILS), (sums_s, SLABS))):
        others = buffer.at[pl.ds(0, size - 1)]
        pltpu.make_async_copy(others, others, sum_send.at[which]).wait()


def per_device(image_est, coil_maps, kernel_tiles, tile_ids, tile_count, measured):
    hbm = pl.BlockSpec(memory_space=pl.ANY)
    vmem = pl.BlockSpec(memory_space=pltpu.VMEM)
    smem = pl.BlockSpec(memory_space=pltpu.SMEM)
    tables = [
        jnp.asarray(x_table()),
        jnp.asarray(long_table(0, 0)),
        jnp.asarray(long_table(FREQ // 2, IMG // 2)),
        jnp.asarray(place_table()),
    ]
    residual, rms = pl.pallas_call(
        kernel,
        out_shape=(
            pltpu.VMEM((1, 2, SLOTS, LANES), F32),
            jax.ShapeDtypeStruct((1,), F32),
        ),
        in_specs=[hbm] * 10,
        out_specs=(vmem, smem),
        scratch_shapes=[
            pltpu.VMEM((8, 2, PLANES, YB, IMG), BF16),
            pltpu.VMEM((2, PLANES, IMG, IMG), BF16),
            pltpu.VMEM((SLOTS, LANES, 256), BF16),
            pltpu.SMEM((SLOTS,), jnp.int32),
            pltpu.SMEM((1,), jnp.int32),
            pltpu.VMEM((2, SLOTS, LANES), F32),
            pltpu.VMEM((2 * IMG, 2 * LANES), BF16),
            pltpu.VMEM((FREQ, 6 * IMG), BF16),
            pltpu.VMEM((FREQ, 6 * IMG), BF16),
            pltpu.VMEM((1024, 512), BF16),
            pltpu.VMEM((8, SLABS * PLANES, LANES), F32),
            pltpu.VMEM((8, SLABS * PLANES, LANES), F32),
            pltpu.VMEM((8, FREQ, LANES), F32),
            pltpu.VMEM((8, FREQ, LANES), F32),
            pltpu.VMEM((9, FREQ, LANES), jnp.int16),
            pltpu.VMEM((9, FREQ, LANES), jnp.int16),
            pltpu.VMEM((FREQ, LANES), F32),
            pltpu.VMEM((KZ * 64, 8, LANES), F32),
            pltpu.VMEM((SLOTS * 8, LANES), F32),
            pltpu.VMEM((2, SLOTS, 512), F32),
            pltpu.VMEM((COILS, 8, LANES), F32),
            pltpu.VMEM((SLABS, 8, LANES), F32),
            pltpu.SemaphoreType.DMA((10,)),
            pltpu.SemaphoreType.DMA((2, 4, 2)),
            pltpu.SemaphoreType.DMA((2, 4, 2)),
            pltpu.SemaphoreType.DMA((5,)),
            pltpu.SemaphoreType.DMA((5,)),
            pltpu.SemaphoreType.DMA((4,)),
            pltpu.SemaphoreType.DMA((4,)),
            pltpu.SemaphoreType.DMA((2,)),
            pltpu.SemaphoreType.DMA((2,)),
        ],
        compiler_params=pltpu.CompilerParams(
            collective_id=0, has_side_effects=True, vmem_limit_bytes=56 * 1024 * 1024
        ),
        cost_estimate=pl.CostEstimate(
            flops=6_000_000_000, bytes_accessed=20_000_000, transcendentals=0
        ),
    )(image_est, coil_maps, kernel_tiles, tile_ids, tile_count, measured, *tables)
    return residual, rms


def solution(mesh):
    placed = (
        P(None, "slab", "coil", None),
        P("coil", None, "slab", None, None),
        P("slab", None, None),
        P("slab"),
        P("slab"),
        P("coil", None, "slab", None),
    )
    return jax.shard_map(
        per_device,
        mesh=mesh,
        in_specs=placed,
        out_specs=(P("coil", None, "slab", None), P()),
        check_vma=False,
    )
```

```python
import jax
import jax.numpy as jnp
import ml_dtypes
import numpy as np
from jax import lax
from jax.experimental import pallas as pl
from jax.experimental.pallas import tpu as pltpu
from jax.sharding import PartitionSpec as P

F32 = jnp.float32
BF16 = jnp.bfloat16
MESH = pl.DeviceIdType.MESH

IMG = 256
KXW = 64
FREQ = 512
SLABS = 32
COILS = 8
PLANES = 8
YB = 32
LANES = 128
KZ = 16
SLOTS = 160
STEPS = 32760.0
CHUNKS = ((0, 1, 7), (2, 6), (3, 5), (4,))
FIRST = (0, 3, 5, 7)
ORDER = (0, 1, 7, 2, 6, 3, 5, 4)
GROUPS = ((0, 4), (4, 7), (7, 11))
MEMBERS = ((0, 1, 2), (3, 4), (5, 6, 7))
ENTRY = (0, 1, 2, 4, 5, 7, 8, 9)
FINE = 16.0


def split_table(table):
    table = table.astype(np.float32)
    high = table.astype(ml_dtypes.bfloat16)
    low = (table - high.astype(np.float32)).astype(ml_dtypes.bfloat16)
    return high, low


def angles(rows, cols, row_offset, col_offset):
    index = (np.arange(rows)[:, None] - row_offset) * (np.arange(cols)[None, :] - col_offset)
    return (index % FREQ) * (2.0 * np.pi / FREQ)


def x_table():
    phase = angles(IMG, KXW, IMG // 2, KXW // 2)
    cosine, sine = np.cos(phase) / 4096.0, np.sin(phase) / 4096.0
    table = np.block([[cosine, -sine], [sine, cosine]])
    high, low = split_table(table)
    return np.concatenate([high, low], axis=1)


def long_table(row_offset, col_offset):
    phase = angles(FREQ, IMG, row_offset, col_offset)
    high, low = split_table(np.concatenate([np.cos(phase), np.sin(phase)], axis=1))
    return np.concatenate([high, high, low], axis=1)


def y_table():
    phase = angles(FREQ, IMG, FREQ // 2, IMG // 2)
    cosine, sine = np.cos(phase), np.sin(phase)
    tables = []
    for coil in range(COILS):
        parts = []
        for half in range(2):
            blocks = [(coil + slot) % COILS for slot in ORDER[4 * half : 4 * half + 4]]
            columns = np.concatenate([np.arange(YB) + YB * block for block in blocks])
            high, low = split_table(np.concatenate([cosine[:, columns], sine[:, columns]], axis=1))
            parts += [high, low]
        tables.append(np.concatenate(parts, axis=1))
    return np.stack(tables)


def place_table():
    table = np.zeros((8, 2, 64, 2, 256), np.float32)
    for w in range(8):
        for part in range(2):
            for u in range(4):
                for v in range(8):
                    table[w, part, 8 * u + v, part, 64 * u + 8 * v + w] = 1.0
    return table.reshape(1024, 512).astype(ml_dtypes.bfloat16)


def split(value):
    high = value.astype(BF16)
    low = (value - high.astype(F32)).astype(BF16)
    return high, low


def kernel(
    img_hbm, maps_hbm, kern_hbm, ids_hbm, count_hbm, meas_hbm, tx_hbm, ez_hbm, ey_hbm, place_hbm,
    res, rms,
    img, maps, kern, ids, count, meas, tx, ez, ey, place,
    send_a, lines, send_b, planes, send_q, coded, power, scale, grid, picked, cells,
    sums_x, sums_y, sums_z,
    load_sem, ring_send, ring_recv, a_send, a_recv, b_send, b_recv, sum_send, sum_recv,
):
    me = lax.axis_index("slab")
    coil = lax.axis_index("coil")
    left = lax.rem(coil + COILS - 1, COILS)
    right = lax.rem(coil + 1, COILS)

    def load(index, src, dst):
        copy = pltpu.make_async_copy(src, dst, load_sem.at[index])
        copy.start()
        return copy

    barrier = pltpu.get_barrier_semaphore()

    @pl.loop(1, SLABS)
    def _(step):
        pl.semaphore_signal(
            barrier, inc=1, device_id={"slab": lax.rem(me + step, SLABS)}, device_id_type=MESH
        )

    @pl.loop(1, COILS)
    def _(step):
        pl.semaphore_signal(
            barrier, inc=1, device_id={"coil": lax.rem(coil + step, COILS)}, device_id_type=MESH
        )

    load_img = load(0, img_hbm, img.at[0])
    load_maps = load(1, maps_hbm.at[0], maps)
    load_tx = load(2, tx_hbm, tx)
    pl.semaphore_wait(barrier, SLABS - 1 + COILS - 1)

    def hop(direction, step, part):
        target = left if direction == 0 else right
        dst_slot = step if direction == 0 else 8 - step
        src_slot = (dst_slot - 1) if direction == 0 else (dst_slot + 1) % 8
        src = img_hbm.at[part] if step == 1 else img.at[src_slot, part]
        return pltpu.make_async_remote_copy(
            src_ref=src,
            dst_ref=img.at[dst_slot, part],
            send_sem=ring_send.at[direction, step - 1, part],
            recv_sem=ring_recv.at[direction, step - 1, part],
            device_id={"coil": target},
            device_id_type=MESH,
        )

    hops = {}
    for direction in range(2):
        for step in range(1, 5):
            for part in range(2):
                if step < 4 or part == direction:
                    hops[direction, step, part] = hop(direction, step, part)

    for part in range(2):
        for direction in range(2):
            hops[direction, 1, part].start()

    load_ez = load(3, ez_hbm, ez)
    late_loads = [
        load(4, ey_hbm.at[coil], ey),
        load(5, place_hbm, place),
        load(6, kern_hbm, kern),
        load(7, ids_hbm, ids),
        load(8, count_hbm, count),
        load(9, meas_hbm.at[0], meas),
    ]

    def arrive(step):
        for part in range(2):
            for direction in range(2):
                if (direction, step, part) in hops:
                    hops[direction, step, part].wait_recv()
                    if (direction, step + 1, part) in hops:
                        hops[direction, step + 1, part].start()

    lane = lax.broadcasted_iota(jnp.int32, (1, LANES), 1)
    sign = jnp.where(lane < 64, 1.0, -1.0).astype(F32)

    def along_x(slot, entry):
        block = lax.rem(coil + slot, COILS)
        rows = pl.ds(pl.multiple_of(block * YB, YB), YB)
        ar = img[slot, 0].astype(F32)
        ai = img[slot, 1].astype(F32)
        sr = maps[0, :, rows, :].astype(F32)
        si = maps[1, :, rows, :].astype(F32)
        wr = (ar * sr - ai * si).reshape(PLANES * YB, IMG)
        wi = (ar * si + ai * sr).reshape(PLANES * YB, IMG)
        high, low = split(jnp.concatenate([wr, wi], axis=1))
        both = jnp.dot(high, tx[...], preferred_element_type=F32)
        out = both[:, :LANES] + both[:, LANES:]
        out = out + jnp.dot(low, tx[:, :LANES], preferred_element_type=F32)
        for z in range(PLANES):
            send_a[entry, pl.ds(z, YB, stride=PLANES), :] = out[z * YB : (z + 1) * YB]

    def exchange(src, dst, first, number, width, send_sem, recv_sem):
        entries = pl.ds(first, number)
        mine = pl.ds(pl.multiple_of(me * width, width), width)

        @pl.loop(1, SLABS)
        def _(step):
            peer = lax.rem(me + step, SLABS)
            theirs = pl.ds(pl.multiple_of(peer * width, width), width)
            pltpu.make_async_remote_copy(
                src_ref=src.at[entries, theirs],
                dst_ref=dst.at[entries, mine],
                send_sem=send_sem,
                recv_sem=recv_sem,
                device_id={"slab": peer},
                device_id_type=MESH,
            ).start()

        dst[entries, mine, :] = src[entries, mine, :]

    def wait_all(ref, number, width, sem):
        part = ref.at[pl.ds(0, number), pl.ds(0, (SLABS - 1) * width)]
        pltpu.make_async_copy(part, part, sem).wait()

    def turned(value):
        swapped = [
            sign * pltpu.roll(value[:, i : i + LANES], 64, 1) for i in range(0, value.shape[1], LANES)
        ]
        return jnp.concatenate([value, jnp.concatenate(swapped, axis=1)], axis=0)

    def transform_half(half, value):
        high, low = split(turned(value))
        table_high = ey[:, 512 * half : 512 * half + 256]
        table_low = ey[:, 512 * half + 256 : 512 * half + 512]
        out = jnp.dot(table_high, high, preferred_element_type=F32)
        out = out + jnp.dot(table_high, low, preferred_element_type=F32)
        return out + jnp.dot(table_low, high, preferred_element_type=F32)

    def transform(table, value):
        high, low = split(turned(value))
        return jnp.dot(
            table[...], jnp.concatenate([high, low, high], axis=0), preferred_element_type=F32
        )

    def stage_x(chunk):
        for i, slot in enumerate(CHUNKS[chunk]):
            if slot:
                along_x(slot, FIRST[chunk] + i)
        number = len(CHUNKS[chunk])
        exchange(
            send_a, lines, FIRST[chunk], number, PLANES, a_send.at[chunk], a_recv.at[chunk]
        )

    def stage_z(chunk):
        number = len(CHUNKS[chunk])
        first = FIRST[chunk]
        wait_all(lines, number, PLANES, a_recv.at[chunk])
        value = jnp.concatenate([lines[first + i] for i in range(number)], axis=1)
        out = transform(ez, value)
        for i in range(number):
            send_b[first + i] = out[:, i * LANES : (i + 1) * LANES]

        @pl.loop(0, SLABS, unroll=4)
        def _(owner):
            rows = pl.ds(pl.multiple_of(owner * KZ, KZ), KZ)
            for i in range(number):
                block = send_b[first + i, rows, :]
                top = jnp.maximum(jnp.max(jnp.abs(block), axis=0, keepdims=True), 1e-30)
                exponent = jnp.ceil(jnp.log2(top) * FINE)
                factor = jnp.exp2(exponent * (-1.0 / FINE)) * STEPS
                send_q[ENTRY[first + i], rows, :] = jnp.round(block * factor).astype(jnp.int16)
                power[pl.ds(owner * KZ + first + i, 1), :] = exponent

    def stage_send(group):
        start, stop = GROUPS[group]
        send_q[stop - 1] = power[...].astype(jnp.int16)
        exchange(send_q, coded, start, stop - start, KZ, b_send.at[group], b_recv.at[group])

    power[...] = jnp.zeros((FREQ, LANES), F32)
    load_img.wait()
    load_maps.wait()
    load_tx.wait()
    along_x(0, 0)
    load_ez.wait()
    arrive(1)
    stage_x(0)
    arrive(2)
    stage_x(1)
    stage_z(0)
    stage_send(0)
    arrive(3)
    stage_x(2)
    arrive(4)
    stage_x(3)
    stage_z(1)
    stage_send(1)
    stage_z(2)
    stage_z(3)
    stage_send(2)
    for copy in late_loads:
        copy.wait()

    def decode(group):
        start, stop = GROUPS[group]
        wait_all(coded, stop - start, KZ, b_recv.at[group])
        scale[...] = jnp.exp2(coded[stop - 1].astype(F32) * (1.0 / FINE)) * (1.0 / STEPS)

        @pl.loop(0, SLABS, unroll=4)
        def _(source):
            rows = pl.ds(pl.multiple_of(source * KZ, KZ), KZ)
            for member in MEMBERS[group]:
                factor = scale[pl.ds(source * KZ + member, 1), :]
                planes[member, rows, :] = coded[ENTRY[member], rows, :].astype(F32) * factor

    def along_y(half):
        @pl.loop(0, KZ // 2)
        def _(pair):
            sides = []
            for odd in range(2):
                rows = pl.ds(2 * pair + odd, SLABS, stride=KZ)
                sides.append(
                    jnp.concatenate(
                        [planes[4 * half + i, rows, :] for i in range(4)], axis=0
                    )
                )
            out = transform_half(half, jnp.concatenate(sides, axis=1))
            for odd in range(2):
                side = out[:, odd * LANES : (odd + 1) * LANES].reshape(64, 8, LANES)
                place_here = pl.ds((2 * pair + odd) * 64, 64)
                if half:
                    side = side + grid[place_here]
                grid[place_here] = side

    decode(0)
    decode(1)
    along_y(0)
    decode(2)
    along_y(1)

    place_of = lax.broadcasted_iota(jnp.int32, (8, LANES), 1) // 8

    @pl.loop(0, SLOTS // 32)
    def _(index):
        found = []
        for k in range(32):
            tile = ids[index * 32 + k]
            first = (tile >> 9) * 256 + (tile & 63)
            b = jnp.full((8, LANES), (tile >> 6) & 7, jnp.int32)
            away = (place_of - b) & 7
            total = jnp.zeros((8, LANES), F32)
            for u in range(4):
                value = grid[first + 64 * u]
                total = jnp.where(away == u, pltpu.roll(value, 8 * u, 1) if u else value, total)
            for bit in (1, 2, 4):
                total = jnp.where((b & bit) > 0, pltpu.roll(total, LANES - 8 * bit, 1), total)
            found.append(total)
        picked[pl.ds(pl.multiple_of(index * 256, 256), 256), :] = jnp.concatenate(found, axis=0)

    high_sum = jnp.zeros((SLOTS, 512), F32)
    low_sum = jnp.zeros((SLOTS, 512), F32)
    for w in range(8):
        high, low = split(picked[pl.ds(w, SLOTS, stride=8), :])
        spot = place[w * LANES : (w + 1) * LANES, :]
        high_sum = high_sum + jnp.dot(high, spot, preferred_element_type=F32)
        low_sum = low_sum + jnp.dot(low, spot, preferred_element_type=F32)
    cells[0] = high_sum
    cells[1] = low_sum

    live = count[0]
    row = lax.broadcasted_iota(jnp.int32, (8, LANES), 0)
    row4 = lax.rem(lax.broadcasted_iota(jnp.int32, (32, LANES), 0), 8)

    def degrid(index, squares):
        first = pl.multiple_of(index * 8, 8)
        rows = pl.ds(first, 8)
        left_side = jnp.concatenate(
            [
                cells[0, rows, :256], cells[1, rows, :256],
                cells[0, rows, 256:], cells[1, rows, 256:],
            ],
            axis=0,
        ).astype(BF16)
        total = jnp.zeros((32, LANES), F32)
        for s in range(0, 8, 2):
            product = lax.dot_general(
                left_side,
                kern[pl.ds(first + s, 2)].reshape(2 * LANES, 256),
                (((1,), (1,)), ((), ())),
                preferred_element_type=F32,
            )
            total = jnp.where(row4 == s, product[:, :LANES], total)
            total = jnp.where(row4 == s + 1, product[:, LANES:], total)
        alive = first + row < live
        for part in range(2):
            predicted = total[16 * part : 16 * part + 8] + total[16 * part + 8 : 16 * part + 16]
            value = jnp.where(alive, predicted - meas[part, rows, :], 0.0)
            res[0, part, rows, :] = value
            squares = squares + value * value
        return squares

    squares = lax.fori_loop(0, SLOTS // 8, degrid, jnp.zeros((8, LANES), F32))

    def total_over(which, buffer, size, position, axis, peer_of, value):
        buffer[position] = value

        @pl.loop(1, size)
        def _(step):
            pltpu.make_async_remote_copy(
                src_ref=buffer.at[position],
                dst_ref=buffer.at[position],
                send_sem=sum_send.at[which],
                recv_sem=sum_recv.at[which],
                device_id={axis: peer_of(lax.rem(position + step, size))},
                device_id_type=MESH,
            ).start()

        others = buffer.at[pl.ds(0, size - 1)]
        pltpu.make_async_copy(others, others, sum_recv.at[which]).wait()
        return jnp.sum(buffer[...], axis=0)

    inner, outer = lax.rem(me, 8), me // 8
    rounds = (
        (sums_x, 8, inner, "slab", lambda k: outer * 8 + k),
        (sums_y, 4, outer, "slab", lambda k: k * 8 + inner),
        (sums_z, COILS, coil, "coil", lambda k: k),
    )
    for which, (buffer, size, position, axis, peer_of) in enumerate(rounds):
        squares = total_over(which, buffer, size, position, axis, peer_of, squares)
    total = jnp.sum(jnp.sum(squares, axis=1, keepdims=True), axis=0, keepdims=True)
    root = jnp.sqrt(total * (1.0 / (COILS * 2 * SLABS * SLOTS * LANES)))
    rms[0] = root[0, 0]

    for copy in hops.values():
        copy.wait_send()
    for chunk in range(len(CHUNKS)):
        wait_all(send_a, len(CHUNKS[chunk]), PLANES, a_send.at[chunk])
    for group, (start, stop) in enumerate(GROUPS):
        wait_all(send_q, stop - start, KZ, b_send.at[group])
    for which, (buffer, size, *_) in enumerate(rounds):
        others = buffer.at[pl.ds(0, size - 1)]
        pltpu.make_async_copy(others, others, sum_send.at[which]).wait()


def per_device(image_est, coil_maps, kernel_tiles, tile_ids, tile_count, measured):
    hbm = pl.BlockSpec(memory_space=pl.ANY)
    vmem = pl.BlockSpec(memory_space=pltpu.VMEM)
    smem = pl.BlockSpec(memory_space=pltpu.SMEM)
    tables = [
        jnp.asarray(x_table()),
        jnp.asarray(long_table(0, 0)),
        jnp.asarray(y_table()),
        jnp.asarray(place_table()),
    ]
    residual, rms = pl.pallas_call(
        kernel,
        out_shape=(
            pltpu.VMEM((1, 2, SLOTS, LANES), F32),
            jax.ShapeDtypeStruct((1,), F32),
        ),
        in_specs=[hbm] * 10,
        out_specs=(vmem, smem),
        scratch_shapes=[
            pltpu.VMEM((8, 2, PLANES, YB, IMG), BF16),
            pltpu.VMEM((2, PLANES, IMG, IMG), BF16),
            pltpu.VMEM((SLOTS, LANES, 256), BF16),
            pltpu.SMEM((SLOTS,), jnp.int32),
            pltpu.SMEM((1,), jnp.int32),
            pltpu.VMEM((2, SLOTS, LANES), F32),
            pltpu.VMEM((2 * IMG, 2 * LANES), BF16),
            pltpu.VMEM((FREQ, 6 * IMG), BF16),
            pltpu.VMEM((FREQ, 4 * IMG), BF16),
            pltpu.VMEM((1024, 512), BF16),
            pltpu.VMEM((8, SLABS * PLANES, LANES), F32),
            pltpu.VMEM((8, SLABS * PLANES, LANES), F32),
            pltpu.VMEM((8, FREQ, LANES), F32),
            pltpu.VMEM((8, FREQ, LANES), F32),
            pltpu.VMEM((11, FREQ, LANES), jnp.int16),
            pltpu.VMEM((11, FREQ, LANES), jnp.int16),
            pltpu.VMEM((FREQ, LANES), F32),
            pltpu.VMEM((FREQ, LANES), F32),
            pltpu.VMEM((KZ * 64, 8, LANES), F32),
            pltpu.VMEM((SLOTS * 8, LANES), F32),
            pltpu.VMEM((2, SLOTS, 512), F32),
            pltpu.VMEM((8, 8, LANES), F32),
            pltpu.VMEM((4, 8, LANES), F32),
            pltpu.VMEM((COILS, 8, LANES), F32),
            pltpu.SemaphoreType.DMA((10,)),
            pltpu.SemaphoreType.DMA((2, 4, 2)),
            pltpu.SemaphoreType.DMA((2, 4, 2)),
            pltpu.SemaphoreType.DMA((4,)),
            pltpu.SemaphoreType.DMA((4,)),
            pltpu.SemaphoreType.DMA((3,)),
            pltpu.SemaphoreType.DMA((3,)),
            pltpu.SemaphoreType.DMA((3,)),
            pltpu.SemaphoreType.DMA((3,)),
        ],
        compiler_params=pltpu.CompilerParams(
            collective_id=0, has_side_effects=True, vmem_limit_bytes=56 * 1024 * 1024
        ),
        cost_estimate=pl.CostEstimate(
            flops=6_000_000_000, bytes_accessed=20_000_000, transcendentals=0
        ),
    )(image_est, coil_maps, kernel_tiles, tile_ids, tile_count, measured, *tables)
    return residual, rms


def solution(mesh):
    placed = (
        P(None, "slab", "coil", None),
        P("coil", None, "slab", None, None),
        P("slab", None, None),
        P("slab"),
        P("slab"),
        P("coil", None, "slab", None),
    )
    return jax.shard_map(
        per_device,
        mesh=mesh,
        in_specs=placed,
        out_specs=(P("coil", None, "slab", None), P()),
        check_vma=False,
    )
```

```python
import jax
import jax.numpy as jnp
import ml_dtypes
import numpy as np
from jax import lax
from jax.experimental import pallas as pl
from jax.experimental.pallas import tpu as pltpu
from jax.sharding import PartitionSpec as P

F32 = jnp.float32
BF16 = jnp.bfloat16
MESH = pl.DeviceIdType.MESH

IMG = 256
KXW = 64
FREQ = 512
SLABS = 32
COILS = 8
PLANES = 8
YB = 32
LANES = 128
KZ = 16
SLOTS = 160
STEPS = 32760.0
CHUNKS = ((0, 1, 7), (2, 6), (3, 5), (4,))
FIRST = (0, 3, 5, 7)
ORDER = (0, 1, 7, 2, 6, 3, 5, 4)
GROUPS = ((0, 4), (4, 7), (7, 11))
MEMBERS = ((0, 1, 2), (3, 4), (5, 6, 7))
ENTRY = (0, 1, 2, 4, 5, 7, 8, 9)
FINE = 16.0


def split_table(table):
    table = table.astype(np.float32)
    high = table.astype(ml_dtypes.bfloat16)
    low = (table - high.astype(np.float32)).astype(ml_dtypes.bfloat16)
    return high, low


def angles(rows, cols, row_offset, col_offset):
    index = (np.arange(rows)[:, None] - row_offset) * (np.arange(cols)[None, :] - col_offset)
    return (index % FREQ) * (2.0 * np.pi / FREQ)


def x_table():
    phase = angles(IMG, KXW, IMG // 2, KXW // 2)
    cosine, sine = np.cos(phase) / 4096.0, np.sin(phase) / 4096.0
    table = np.block([[cosine, -sine], [sine, cosine]])
    high, low = split_table(table)
    return np.concatenate([high, low], axis=1)


def long_table(row_offset, col_offset):
    phase = angles(FREQ, IMG, row_offset, col_offset)
    high, low = split_table(np.concatenate([np.cos(phase), np.sin(phase)], axis=1))
    return np.concatenate([high, high, low], axis=1)


def y_table():
    phase = angles(FREQ, IMG, FREQ // 2, IMG // 2)
    cosine, sine = np.cos(phase), np.sin(phase)
    tables = []
    for coil in range(COILS):
        parts = []
        for half in range(2):
            blocks = [(coil + slot) % COILS for slot in ORDER[4 * half : 4 * half + 4]]
            columns = np.concatenate([np.arange(YB) + YB * block for block in blocks])
            high, low = split_table(np.concatenate([cosine[:, columns], sine[:, columns]], axis=1))
            parts += [high, low]
        tables.append(np.concatenate(parts, axis=1))
    return np.stack(tables)


def place_table():
    table = np.zeros((8, 2, 64, 2, 256), np.float32)
    for w in range(8):
        for part in range(2):
            for u in range(4):
                for v in range(8):
                    table[w, part, 8 * u + v, part, 64 * u + 8 * v + w] = 1.0
    return table.reshape(1024, 512).astype(ml_dtypes.bfloat16)


def split(value):
    high = value.astype(BF16)
    low = (value - high.astype(F32)).astype(BF16)
    return high, low


def kernel(
    img_hbm, maps_hbm, kern_hbm, ids_hbm, count_hbm, meas_hbm, tx_hbm, ez_hbm, ey_hbm, place_hbm,
    res, rms,
    img, maps, kern, ids, count, meas, tx, ez, ey, place,
    send_a, lines, send_b, planes, send_q, coded, power, scale, grid, picked, cells,
    sums_x, sums_y, sums_z,
    load_sem, ring_send, ring_recv, a_send, a_recv, b_send, b_recv, sum_send, sum_recv,
):
    me = lax.axis_index("slab")
    coil = lax.axis_index("coil")
    left = lax.rem(coil + COILS - 1, COILS)
    right = lax.rem(coil + 1, COILS)

    def load(index, src, dst):
        copy = pltpu.make_async_copy(src, dst, load_sem.at[index])
        copy.start()
        return copy

    barrier = pltpu.get_barrier_semaphore()

    @pl.loop(1, SLABS)
    def _(step):
        pl.semaphore_signal(
            barrier, inc=1, device_id={"slab": lax.rem(me + step, SLABS)}, device_id_type=MESH
        )

    @pl.loop(1, COILS)
    def _(step):
        pl.semaphore_signal(
            barrier, inc=1, device_id={"coil": lax.rem(coil + step, COILS)}, device_id_type=MESH
        )

    load_img = load(0, img_hbm, img.at[0])
    load_maps = load(1, maps_hbm.at[0], maps)
    load_tx = load(2, tx_hbm, tx)
    pl.semaphore_wait(barrier, SLABS - 1 + COILS - 1)

    def hop(direction, step, part):
        target = left if direction == 0 else right
        dst_slot = step if direction == 0 else 8 - step
        src_slot = (dst_slot - 1) if direction == 0 else (dst_slot + 1) % 8
        src = img_hbm.at[part] if step == 1 else img.at[src_slot, part]
        return pltpu.make_async_remote_copy(
            src_ref=src,
            dst_ref=img.at[dst_slot, part],
            send_sem=ring_send.at[direction, step - 1, part],
            recv_sem=ring_recv.at[direction, step - 1, part],
            device_id={"coil": target},
            device_id_type=MESH,
        )

    hops = {}
    for direction in range(2):
        for step in range(1, 5):
            for part in range(2):
                if step < 4 or part == direction:
                    hops[direction, step, part] = hop(direction, step, part)

    for part in range(2):
        for direction in range(2):
            hops[direction, 1, part].start()

    load_ez = load(3, ez_hbm, ez)
    late_loads = [
        load(4, ey_hbm.at[coil], ey),
        load(5, place_hbm, place),
        load(6, kern_hbm, kern),
        load(7, ids_hbm, ids),
        load(8, count_hbm, count),
        load(9, meas_hbm.at[0], meas),
    ]

    def arrive(step):
        for part in range(2):
            for direction in range(2):
                if (direction, step, part) in hops:
                    hops[direction, step, part].wait_recv()
                    if (direction, step + 1, part) in hops:
                        hops[direction, step + 1, part].start()

    lane = lax.broadcasted_iota(jnp.int32, (1, LANES), 1)
    sign = jnp.where(lane < 64, 1.0, -1.0).astype(F32)

    def along_x(slot, entry):
        block = lax.rem(coil + slot, COILS)
        rows = pl.ds(pl.multiple_of(block * YB, YB), YB)
        ar = img[slot, 0].astype(F32)
        ai = img[slot, 1].astype(F32)
        sr = maps[0, :, rows, :].astype(F32)
        si = maps[1, :, rows, :].astype(F32)
        wr = (ar * sr - ai * si).reshape(PLANES * YB, IMG)
        wi = (ar * si + ai * sr).reshape(PLANES * YB, IMG)
        high, low = split(jnp.concatenate([wr, wi], axis=1))
        both = jnp.dot(high, tx[...], preferred_element_type=F32)
        out = both[:, :LANES] + both[:, LANES:]
        out = out + jnp.dot(low, tx[:, :LANES], preferred_element_type=F32)
        for z in range(PLANES):
            send_a[entry, pl.ds(z, YB, stride=PLANES), :] = out[z * YB : (z + 1) * YB]

    def exchange(src, dst, first, number, width, send_sem, recv_sem):
        entries = pl.ds(first, number)
        mine = pl.ds(pl.multiple_of(me * width, width), width)

        @pl.loop(1, SLABS)
        def _(step):
            peer = lax.rem(me + step, SLABS)
            theirs = pl.ds(pl.multiple_of(peer * width, width), width)
            pltpu.make_async_remote_copy(
                src_ref=src.at[entries, theirs],
                dst_ref=dst.at[entries, mine],
                send_sem=send_sem,
                recv_sem=recv_sem,
                device_id={"slab": peer},
                device_id_type=MESH,
            ).start()

        dst[entries, mine, :] = src[entries, mine, :]

    def wait_all(ref, number, width, sem):
        part = ref.at[pl.ds(0, number), pl.ds(0, (SLABS - 1) * width)]
        pltpu.make_async_copy(part, part, sem).wait()

    def turned(value):
        swapped = [
            sign * pltpu.roll(value[:, i : i + LANES], 64, 1) for i in range(0, value.shape[1], LANES)
        ]
        return jnp.concatenate([value, jnp.concatenate(swapped, axis=1)], axis=0)

    def transform_half(half, value):
        high, low = split(turned(value))
        table_high = ey[:, 512 * half : 512 * half + 256]
        table_low = ey[:, 512 * half + 256 : 512 * half + 512]
        out = jnp.dot(table_high, high, preferred_element_type=F32)
        out = out + jnp.dot(table_high, low, preferred_element_type=F32)
        return out + jnp.dot(table_low, high, preferred_element_type=F32)

    def transform(table, value):
        high, low = split(turned(value))
        return jnp.dot(
            table[...], jnp.concatenate([high, low, high], axis=0), preferred_element_type=F32
        )

    def stage_x(chunk):
        for i, slot in enumerate(CHUNKS[chunk]):
            if slot:
                along_x(slot, FIRST[chunk] + i)
        number = len(CHUNKS[chunk])
        exchange(
            send_a, lines, FIRST[chunk], number, PLANES, a_send.at[chunk], a_recv.at[chunk]
        )

    def stage_z(chunk):
        number = len(CHUNKS[chunk])
        first = FIRST[chunk]
        wait_all(lines, number, PLANES, a_recv.at[chunk])
        value = jnp.concatenate([lines[first + i] for i in range(number)], axis=1)
        out = transform(ez, value)
        for i in range(number):
            send_b[first + i] = out[:, i * LANES : (i + 1) * LANES]

        @pl.loop(0, SLABS, unroll=8)
        def _(owner):
            rows = pl.ds(pl.multiple_of(owner * KZ, KZ), KZ)
            for i in range(number):
                block = send_b[first + i, rows, :]
                top = jnp.maximum(jnp.max(jnp.abs(block), axis=0, keepdims=True), 1e-30)
                exponent = jnp.ceil(jnp.log2(top) * FINE)
                factor = jnp.exp2(exponent * (-1.0 / FINE)) * STEPS
                send_q[ENTRY[first + i], rows, :] = jnp.round(block * factor).astype(jnp.int16)
                power[pl.ds(owner * KZ + first + i, 1), :] = exponent

    def stage_send(group):
        start, stop = GROUPS[group]
        send_q[stop - 1] = power[...].astype(jnp.int16)
        exchange(send_q, coded, start, stop - start, KZ, b_send.at[group], b_recv.at[group])

    power[...] = jnp.zeros((FREQ, LANES), F32)
    load_img.wait()
    load_maps.wait()
    load_tx.wait()
    along_x(0, 0)
    load_ez.wait()
    arrive(1)
    stage_x(0)
    arrive(2)
    stage_x(1)
    stage_z(0)
    stage_send(0)
    arrive(3)
    stage_x(2)
    arrive(4)
    stage_x(3)
    stage_z(1)
    stage_send(1)
    stage_z(2)
    stage_z(3)
    stage_send(2)
    for copy in late_loads:
        copy.wait()

    def decode(group):
        start, stop = GROUPS[group]
        wait_all(coded, stop - start, KZ, b_recv.at[group])
        scale[...] = jnp.exp2(coded[stop - 1].astype(F32) * (1.0 / FINE)) * (1.0 / STEPS)

        @pl.loop(0, SLABS, unroll=8)
        def _(source):
            rows = pl.ds(pl.multiple_of(source * KZ, KZ), KZ)
            for member in MEMBERS[group]:
                factor = scale[pl.ds(source * KZ + member, 1), :]
                planes[member, rows, :] = coded[ENTRY[member], rows, :].astype(F32) * factor

    def along_y(half):
        @pl.loop(0, KZ // 2, unroll=4)
        def _(pair):
            sides = []
            for odd in range(2):
                rows = pl.ds(2 * pair + odd, SLABS, stride=KZ)
                sides.append(
                    jnp.concatenate(
                        [planes[4 * half + i, rows, :] for i in range(4)], axis=0
                    )
                )
            out = transform_half(half, jnp.concatenate(sides, axis=1))
            for odd in range(2):
                side = out[:, odd * LANES : (odd + 1) * LANES].reshape(64, 8, LANES)
                place_here = pl.ds((2 * pair + odd) * 64, 64)
                if half:
                    side = side + grid[place_here]
                grid[place_here] = side

    decode(0)
    decode(1)
    along_y(0)
    decode(2)
    along_y(1)

    place_of = lax.broadcasted_iota(jnp.int32, (8, LANES), 1) // 8

    @pl.loop(0, SLOTS // 32, unroll=5)
    def _(index):
        found = []
        for k in range(32):
            tile = ids[index * 32 + k]
            first = (tile >> 9) * 256 + (tile & 63)
            b = jnp.full((8, LANES), (tile >> 6) & 7, jnp.int32)
            away = (place_of - b) & 7
            total = jnp.zeros((8, LANES), F32)
            for u in range(4):
                value = grid[first + 64 * u]
                total = jnp.where(away == u, pltpu.roll(value, 8 * u, 1) if u else value, total)
            for bit in (1, 2, 4):
                total = jnp.where((b & bit) > 0, pltpu.roll(total, LANES - 8 * bit, 1), total)
            found.append(total)
        picked[pl.ds(pl.multiple_of(index * 256, 256), 256), :] = jnp.concatenate(found, axis=0)

    high_sum = jnp.zeros((SLOTS, 512), F32)
    low_sum = jnp.zeros((SLOTS, 512), F32)
    for w in range(8):
        high, low = split(picked[pl.ds(w, SLOTS, stride=8), :])
        spot = place[w * LANES : (w + 1) * LANES, :]
        high_sum = high_sum + jnp.dot(high, spot, preferred_element_type=F32)
        low_sum = low_sum + jnp.dot(low, spot, preferred_element_type=F32)
    cells[0] = high_sum
    cells[1] = low_sum

    live = count[0]
    row = lax.broadcasted_iota(jnp.int32, (8, LANES), 0)
    row4 = lax.rem(lax.broadcasted_iota(jnp.int32, (32, LANES), 0), 8)

    def degrid(index, squares):
        first = pl.multiple_of(index * 8, 8)
        rows = pl.ds(first, 8)
        left_side = jnp.concatenate(
            [
                cells[0, rows, :256], cells[1, rows, :256],
                cells[0, rows, 256:], cells[1, rows, 256:],
            ],
            axis=0,
        ).astype(BF16)
        total = jnp.zeros((32, LANES), F32)
        for s in range(0, 8, 2):
            product = lax.dot_general(
                left_side,
                kern[pl.ds(first + s, 2)].reshape(2 * LANES, 256),
                (((1,), (1,)), ((), ())),
                preferred_element_type=F32,
            )
            total = jnp.where(row4 == s, product[:, :LANES], total)
            total = jnp.where(row4 == s + 1, product[:, LANES:], total)
        alive = first + row < live
        for part in range(2):
            predicted = total[16 * part : 16 * part + 8] + total[16 * part + 8 : 16 * part + 16]
            value = jnp.where(alive, predicted - meas[part, rows, :], 0.0)
            res[0, part, rows, :] = value
            squares = squares + value * value
        return squares

    squares = lax.fori_loop(0, SLOTS // 8, degrid, jnp.zeros((8, LANES), F32), unroll=10)

    def total_over(which, buffer, size, position, axis, peer_of, value):
        buffer[position] = value

        @pl.loop(1, size)
        def _(step):
            pltpu.make_async_remote_copy(
                src_ref=buffer.at[position],
                dst_ref=buffer.at[position],
                send_sem=sum_send.at[which],
                recv_sem=sum_recv.at[which],
                device_id={axis: peer_of(lax.rem(position + step, size))},
                device_id_type=MESH,
            ).start()

        others = buffer.at[pl.ds(0, size - 1)]
        pltpu.make_async_copy(others, others, sum_recv.at[which]).wait()
        return jnp.sum(buffer[...], axis=0)

    inner, outer = lax.rem(me, 8), me // 8
    rounds = (
        (sums_x, 8, inner, "slab", lambda k: outer * 8 + k),
        (sums_y, 4, outer, "slab", lambda k: k * 8 + inner),
        (sums_z, COILS, coil, "coil", lambda k: k),
    )
    for which, (buffer, size, position, axis, peer_of) in enumerate(rounds):
        squares = total_over(which, buffer, size, position, axis, peer_of, squares)
    total = jnp.sum(jnp.sum(squares, axis=1, keepdims=True), axis=0, keepdims=True)
    root = jnp.sqrt(total * (1.0 / (COILS * 2 * SLABS * SLOTS * LANES)))
    rms[0] = root[0, 0]

    for copy in hops.values():
        copy.wait_send()
    for chunk in range(len(CHUNKS)):
        wait_all(send_a, len(CHUNKS[chunk]), PLANES, a_send.at[chunk])
    for group, (start, stop) in enumerate(GROUPS):
        wait_all(send_q, stop - start, KZ, b_send.at[group])
    for which, (buffer, size, *_) in enumerate(rounds):
        others = buffer.at[pl.ds(0, size - 1)]
        pltpu.make_async_copy(others, others, sum_send.at[which]).wait()


def per_device(image_est, coil_maps, kernel_tiles, tile_ids, tile_count, measured):
    hbm = pl.BlockSpec(memory_space=pl.ANY)
    vmem = pl.BlockSpec(memory_space=pltpu.VMEM)
    smem = pl.BlockSpec(memory_space=pltpu.SMEM)
    tables = [
        jnp.asarray(x_table()),
        jnp.asarray(long_table(0, 0)),
        jnp.asarray(y_table()),
        jnp.asarray(place_table()),
    ]
    residual, rms = pl.pallas_call(
        kernel,
        out_shape=(
            pltpu.VMEM((1, 2, SLOTS, LANES), F32),
            jax.ShapeDtypeStruct((1,), F32),
        ),
        in_specs=[hbm] * 10,
        out_specs=(vmem, smem),
        scratch_shapes=[
            pltpu.VMEM((8, 2, PLANES, YB, IMG), BF16),
            pltpu.VMEM((2, PLANES, IMG, IMG), BF16),
            pltpu.VMEM((SLOTS, LANES, 256), BF16),
            pltpu.SMEM((SLOTS,), jnp.int32),
            pltpu.SMEM((1,), jnp.int32),
            pltpu.VMEM((2, SLOTS, LANES), F32),
            pltpu.VMEM((2 * IMG, 2 * LANES), BF16),
            pltpu.VMEM((FREQ, 6 * IMG), BF16),
            pltpu.VMEM((FREQ, 4 * IMG), BF16),
            pltpu.VMEM((1024, 512), BF16),
            pltpu.VMEM((8, SLABS * PLANES, LANES), F32),
            pltpu.VMEM((8, SLABS * PLANES, LANES), F32),
            pltpu.VMEM((8, FREQ, LANES), F32),
            pltpu.VMEM((8, FREQ, LANES), F32),
            pltpu.VMEM((11, FREQ, LANES), jnp.int16),
            pltpu.VMEM((11, FREQ, LANES), jnp.int16),
            pltpu.VMEM((FREQ, LANES), F32),
            pltpu.VMEM((FREQ, LANES), F32),
            pltpu.VMEM((KZ * 64, 8, LANES), F32),
            pltpu.VMEM((SLOTS * 8, LANES), F32),
            pltpu.VMEM((2, SLOTS, 512), F32),
            pltpu.VMEM((8, 8, LANES), F32),
            pltpu.VMEM((4, 8, LANES), F32),
            pltpu.VMEM((COILS, 8, LANES), F32),
            pltpu.SemaphoreType.DMA((10,)),
            pltpu.SemaphoreType.DMA((2, 4, 2)),
            pltpu.SemaphoreType.DMA((2, 4, 2)),
            pltpu.SemaphoreType.DMA((4,)),
            pltpu.SemaphoreType.DMA((4,)),
            pltpu.SemaphoreType.DMA((3,)),
            pltpu.SemaphoreType.DMA((3,)),
            pltpu.SemaphoreType.DMA((3,)),
            pltpu.SemaphoreType.DMA((3,)),
        ],
        compiler_params=pltpu.CompilerParams(
            collective_id=0, has_side_effects=True, vmem_limit_bytes=56 * 1024 * 1024
        ),
        cost_estimate=pl.CostEstimate(
            flops=6_000_000_000, bytes_accessed=20_000_000, transcendentals=0
        ),
    )(image_est, coil_maps, kernel_tiles, tile_ids, tile_count, measured, *tables)
    return residual, rms


def solution(mesh):
    placed = (
        P(None, "slab", "coil", None),
        P("coil", None, "slab", None, None),
        P("slab", None, None),
        P("slab"),
        P("slab"),
        P("coil", None, "slab", None),
    )
    return jax.shard_map(
        per_device,
        mesh=mesh,
        in_specs=placed,
        out_specs=(P("coil", None, "slab", None), P()),
        check_vma=False,
    )
```

```python
import jax
import jax.numpy as jnp
import ml_dtypes
import numpy as np
from jax import lax
from jax.experimental import pallas as pl
from jax.experimental.pallas import tpu as pltpu
from jax.sharding import PartitionSpec as P

F32 = jnp.float32
BF16 = jnp.bfloat16
MESH = pl.DeviceIdType.MESH

IMG = 256
KXW = 64
FREQ = 512
SLABS = 32
COILS = 8
PLANES = 8
YB = 32
LANES = 128
KZ = 16
SLOTS = 160
STEPS = 32760.0
CHUNKS = ((0, 1, 7), (2, 6), (3, 5), (4,))
FIRST = (0, 3, 5, 7)
ORDER = (0, 1, 7, 2, 6, 3, 5, 4)
GROUPS = ((0, 4), (4, 7), (7, 11))
MEMBERS = ((0, 1, 2), (3, 4), (5, 6, 7))
ENTRY = (0, 1, 2, 4, 5, 7, 8, 9)
FINE = 16.0


def split_table(table):
    table = table.astype(np.float32)
    high = table.astype(ml_dtypes.bfloat16)
    low = (table - high.astype(np.float32)).astype(ml_dtypes.bfloat16)
    return high, low


def angles(rows, cols, row_offset, col_offset):
    index = (np.arange(rows)[:, None] - row_offset) * (np.arange(cols)[None, :] - col_offset)
    return (index % FREQ) * (2.0 * np.pi / FREQ)


def x_table():
    phase = angles(IMG, KXW, IMG // 2, KXW // 2)
    cosine, sine = np.cos(phase) / 4096.0, np.sin(phase) / 4096.0
    table = np.block([[cosine, -sine], [sine, cosine]])
    high, low = split_table(table)
    return np.concatenate([high, low], axis=1)


def long_table(row_offset, col_offset):
    phase = angles(FREQ, IMG, row_offset, col_offset)
    high, low = split_table(np.concatenate([np.cos(phase), np.sin(phase)], axis=1))
    return np.concatenate([high, high, low], axis=1)


def y_table():
    phase = angles(FREQ, IMG, FREQ // 2, IMG // 2)
    cosine, sine = np.cos(phase), np.sin(phase)
    tables = []
    for coil in range(COILS):
        parts = []
        for half in range(2):
            blocks = [(coil + slot) % COILS for slot in ORDER[4 * half : 4 * half + 4]]
            columns = np.concatenate([np.arange(YB) + YB * block for block in blocks])
            high, low = split_table(np.concatenate([cosine[:, columns], sine[:, columns]], axis=1))
            parts += [high, low]
        tables.append(np.concatenate(parts, axis=1))
    return np.stack(tables)


def place_table():
    table = np.zeros((8, 2, 64, 2, 256), np.float32)
    for w in range(8):
        for part in range(2):
            for u in range(4):
                for v in range(8):
                    table[w, part, 8 * u + v, part, 64 * u + 8 * v + w] = 1.0
    return table.reshape(1024, 512).astype(ml_dtypes.bfloat16)


def split(value):
    high = value.astype(BF16)
    low = (value - high.astype(F32)).astype(BF16)
    return high, low


def kernel(
    img_hbm, maps_hbm, kern_hbm, ids_hbm, count_hbm, meas_hbm, tx_hbm, ez_hbm, ey_hbm, place_hbm,
    res, rms,
    img, maps, kern, ids, count, meas, tx, ez, ey, place,
    send_a, lines, send_b, planes, send_q, coded, power, scale, grid, picked, cells,
    sums_z, sums_s,
    load_sem, ring_send, ring_recv, a_send, a_recv, b_send, b_recv, sum_send, sum_recv,
):
    me = lax.axis_index("slab")
    coil = lax.axis_index("coil")
    left = lax.rem(coil + COILS - 1, COILS)
    right = lax.rem(coil + 1, COILS)

    def load(index, src, dst):
        copy = pltpu.make_async_copy(src, dst, load_sem.at[index])
        copy.start()
        return copy

    barrier = pltpu.get_barrier_semaphore()

    @pl.loop(1, SLABS)
    def _(step):
        pl.semaphore_signal(
            barrier, inc=1, device_id={"slab": lax.rem(me + step, SLABS)}, device_id_type=MESH
        )

    @pl.loop(1, COILS)
    def _(step):
        pl.semaphore_signal(
            barrier, inc=1, device_id={"coil": lax.rem(coil + step, COILS)}, device_id_type=MESH
        )

    load_img = load(0, img_hbm, img.at[0])
    load_maps = load(1, maps_hbm.at[0], maps)
    load_tx = load(2, tx_hbm, tx)
    pl.semaphore_wait(barrier, SLABS - 1 + COILS - 1)

    def hop(direction, step, part):
        target = left if direction == 0 else right
        dst_slot = step if direction == 0 else 8 - step
        src_slot = (dst_slot - 1) if direction == 0 else (dst_slot + 1) % 8
        src = img_hbm.at[part] if step == 1 else img.at[src_slot, part]
        return pltpu.make_async_remote_copy(
            src_ref=src,
            dst_ref=img.at[dst_slot, part],
            send_sem=ring_send.at[direction, step - 1, part],
            recv_sem=ring_recv.at[direction, step - 1, part],
            device_id={"coil": target},
            device_id_type=MESH,
        )

    hops = {}
    for direction in range(2):
        for step in range(1, 5):
            for part in range(2):
                if step < 4 or part == direction:
                    hops[direction, step, part] = hop(direction, step, part)

    for part in range(2):
        for direction in range(2):
            hops[direction, 1, part].start()

    load_ez = load(3, ez_hbm, ez)
    late_loads = [
        load(4, ey_hbm.at[coil], ey),
        load(5, place_hbm, place),
        load(6, kern_hbm, kern),
        load(7, ids_hbm, ids),
        load(8, count_hbm, count),
        load(9, meas_hbm.at[0], meas),
    ]

    def arrive(step):
        for part in range(2):
            for direction in range(2):
                if (direction, step, part) in hops:
                    hops[direction, step, part].wait_recv()
                    if (direction, step + 1, part) in hops:
                        hops[direction, step + 1, part].start()

    lane = lax.broadcasted_iota(jnp.int32, (1, LANES), 1)
    sign = jnp.where(lane < 64, 1.0, -1.0).astype(F32)

    def along_x(slot, entry):
        block = lax.rem(coil + slot, COILS)
        rows = pl.ds(pl.multiple_of(block * YB, YB), YB)
        ar = img[slot, 0].astype(F32)
        ai = img[slot, 1].astype(F32)
        sr = maps[0, :, rows, :].astype(F32)
        si = maps[1, :, rows, :].astype(F32)
        wr = (ar * sr - ai * si).reshape(PLANES * YB, IMG)
        wi = (ar * si + ai * sr).reshape(PLANES * YB, IMG)
        high, low = split(jnp.concatenate([wr, wi], axis=1))
        both = jnp.dot(high, tx[...], preferred_element_type=F32)
        out = both[:, :LANES] + both[:, LANES:]
        out = out + jnp.dot(low, tx[:, :LANES], preferred_element_type=F32)
        for z in range(PLANES):
            send_a[entry, pl.ds(z, YB, stride=PLANES), :] = out[z * YB : (z + 1) * YB]

    def exchange(src, dst, first, number, width, send_sem, recv_sem):
        entries = pl.ds(first, number)
        mine = pl.ds(pl.multiple_of(me * width, width), width)

        @pl.loop(1, SLABS)
        def _(step):
            peer = lax.rem(me + step, SLABS)
            theirs = pl.ds(pl.multiple_of(peer * width, width), width)
            pltpu.make_async_remote_copy(
                src_ref=src.at[entries, theirs],
                dst_ref=dst.at[entries, mine],
                send_sem=send_sem,
                recv_sem=recv_sem,
                device_id={"slab": peer},
                device_id_type=MESH,
            ).start()

        dst[entries, mine, :] = src[entries, mine, :]

    def wait_all(ref, number, width, sem):
        part = ref.at[pl.ds(0, number), pl.ds(0, (SLABS - 1) * width)]
        pltpu.make_async_copy(part, part, sem).wait()

    def turned(value):
        swapped = [
            sign * pltpu.roll(value[:, i : i + LANES], 64, 1) for i in range(0, value.shape[1], LANES)
        ]
        return jnp.concatenate([value, jnp.concatenate(swapped, axis=1)], axis=0)

    def transform_half(half, value):
        high, low = split(turned(value))
        table_high = ey[:, 512 * half : 512 * half + 256]
        table_low = ey[:, 512 * half + 256 : 512 * half + 512]
        out = jnp.dot(table_high, high, preferred_element_type=F32)
        out = out + jnp.dot(table_high, low, preferred_element_type=F32)
        return out + jnp.dot(table_low, high, preferred_element_type=F32)

    def transform(table, value):
        high, low = split(turned(value))
        return jnp.dot(
            table[...], jnp.concatenate([high, low, high], axis=0), preferred_element_type=F32
        )

    def stage_x(chunk):
        for i, slot in enumerate(CHUNKS[chunk]):
            if slot:
                along_x(slot, FIRST[chunk] + i)
        number = len(CHUNKS[chunk])
        exchange(
            send_a, lines, FIRST[chunk], number, PLANES, a_send.at[chunk], a_recv.at[chunk]
        )

    def stage_z(chunk):
        number = len(CHUNKS[chunk])
        first = FIRST[chunk]
        wait_all(lines, number, PLANES, a_recv.at[chunk])
        value = jnp.concatenate([lines[first + i] for i in range(number)], axis=1)
        out = transform(ez, value)
        for i in range(number):
            send_b[first + i] = out[:, i * LANES : (i + 1) * LANES]

        @pl.loop(0, SLABS, unroll=8)
        def _(owner):
            rows = pl.ds(pl.multiple_of(owner * KZ, KZ), KZ)
            for i in range(number):
                block = send_b[first + i, rows, :]
                top = jnp.maximum(jnp.max(jnp.abs(block), axis=0, keepdims=True), 1e-30)
                exponent = jnp.ceil(jnp.log2(top) * FINE)
                factor = jnp.exp2(exponent * (-1.0 / FINE)) * STEPS
                send_q[ENTRY[first + i], rows, :] = jnp.round(block * factor).astype(jnp.int16)
                power[pl.ds(owner * KZ + first + i, 1), :] = exponent

    def stage_send(group):
        start, stop = GROUPS[group]
        send_q[stop - 1] = power[...].astype(jnp.int16)
        exchange(send_q, coded, start, stop - start, KZ, b_send.at[group], b_recv.at[group])

    power[...] = jnp.zeros((FREQ, LANES), F32)
    load_img.wait()
    load_maps.wait()
    load_tx.wait()
    along_x(0, 0)
    load_ez.wait()
    arrive(1)
    stage_x(0)
    arrive(2)
    stage_x(1)
    stage_z(0)
    stage_send(0)
    arrive(3)
    stage_x(2)
    arrive(4)
    stage_x(3)
    stage_z(1)
    stage_send(1)
    stage_z(2)
    stage_z(3)
    stage_send(2)
    for copy in late_loads:
        copy.wait()

    def decode(group):
        start, stop = GROUPS[group]
        wait_all(coded, stop - start, KZ, b_recv.at[group])
        scale[...] = jnp.exp2(coded[stop - 1].astype(F32) * (1.0 / FINE)) * (1.0 / STEPS)

        @pl.loop(0, SLABS, unroll=8)
        def _(source):
            rows = pl.ds(pl.multiple_of(source * KZ, KZ), KZ)
            for member in MEMBERS[group]:
                factor = scale[pl.ds(source * KZ + member, 1), :]
                planes[member, rows, :] = coded[ENTRY[member], rows, :].astype(F32) * factor

    def along_y(half):
        @pl.loop(0, KZ // 2, unroll=4)
        def _(pair):
            sides = []
            for odd in range(2):
                rows = pl.ds(2 * pair + odd, SLABS, stride=KZ)
                sides.append(
                    jnp.concatenate(
                        [planes[4 * half + i, rows, :] for i in range(4)], axis=0
                    )
                )
            out = transform_half(half, jnp.concatenate(sides, axis=1))
            for odd in range(2):
                side = out[:, odd * LANES : (odd + 1) * LANES].reshape(64, 8, LANES)
                place_here = pl.ds((2 * pair + odd) * 64, 64)
                if half:
                    side = side + grid[place_here]
                grid[place_here] = side

    decode(0)
    decode(1)
    along_y(0)
    decode(2)
    along_y(1)

    place_of = lax.broadcasted_iota(jnp.int32, (8, LANES), 1) // 8

    @pl.loop(0, SLOTS // 32, unroll=5)
    def _(index):
        found = []
        for k in range(32):
            tile = ids[index * 32 + k]
            first = (tile >> 9) * 256 + (tile & 63)
            b = jnp.full((8, LANES), (tile >> 6) & 7, jnp.int32)
            away = (place_of - b) & 7
            total = jnp.zeros((8, LANES), F32)
            for u in range(4):
                value = grid[first + 64 * u]
                total = jnp.where(away == u, pltpu.roll(value, 8 * u, 1) if u else value, total)
            for bit in (1, 2, 4):
                total = jnp.where((b & bit) > 0, pltpu.roll(total, LANES - 8 * bit, 1), total)
            found.append(total)
        picked[pl.ds(pl.multiple_of(index * 256, 256), 256), :] = jnp.concatenate(found, axis=0)

    high_sum = jnp.zeros((SLOTS, 512), F32)
    low_sum = jnp.zeros((SLOTS, 512), F32)
    for w in range(8):
        high, low = split(picked[pl.ds(w, SLOTS, stride=8), :])
        spot = place[w * LANES : (w + 1) * LANES, :]
        high_sum = high_sum + jnp.dot(high, spot, preferred_element_type=F32)
        low_sum = low_sum + jnp.dot(low, spot, preferred_element_type=F32)
    cells[0] = high_sum
    cells[1] = low_sum

    live = count[0]
    row = lax.broadcasted_iota(jnp.int32, (8, LANES), 0)
    row4 = lax.rem(lax.broadcasted_iota(jnp.int32, (32, LANES), 0), 8)

    def degrid(index, squares):
        first = pl.multiple_of(index * 8, 8)
        rows = pl.ds(first, 8)
        left_side = jnp.concatenate(
            [
                cells[0, rows, :256], cells[1, rows, :256],
                cells[0, rows, 256:], cells[1, rows, 256:],
            ],
            axis=0,
        ).astype(BF16)
        total = jnp.zeros((32, LANES), F32)
        for s in range(0, 8, 2):
            product = lax.dot_general(
                left_side,
                kern[pl.ds(first + s, 2)].reshape(2 * LANES, 256),
                (((1,), (1,)), ((), ())),
                preferred_element_type=F32,
            )
            total = jnp.where(row4 == s, product[:, :LANES], total)
            total = jnp.where(row4 == s + 1, product[:, LANES:], total)
        alive = first + row < live
        for part in range(2):
            predicted = total[16 * part : 16 * part + 8] + total[16 * part + 8 : 16 * part + 16]
            value = jnp.where(alive, predicted - meas[part, rows, :], 0.0)
            res[0, part, rows, :] = value
            squares = squares + value * value
        return squares

    squares = lax.fori_loop(0, SLOTS // 8, degrid, jnp.zeros((8, LANES), F32), unroll=10)

    def total_over(which, buffer, size, position, axis, peer_of, value):
        buffer[position] = value

        @pl.loop(1, size)
        def _(step):
            pltpu.make_async_remote_copy(
                src_ref=buffer.at[position],
                dst_ref=buffer.at[position],
                send_sem=sum_send.at[which],
                recv_sem=sum_recv.at[which],
                device_id={axis: peer_of(lax.rem(position + step, size))},
                device_id_type=MESH,
            ).start()

        others = buffer.at[pl.ds(0, size - 1)]
        pltpu.make_async_copy(others, others, sum_recv.at[which]).wait()
        return jnp.sum(buffer[...], axis=0)

    rounds = (
        (sums_z, COILS, coil, "coil", lambda k: k),
        (sums_s, SLABS, me, "slab", lambda k: k),
    )
    for which, (buffer, size, position, axis, peer_of) in enumerate(rounds):
        squares = total_over(which, buffer, size, position, axis, peer_of, squares)
    total = jnp.sum(jnp.sum(squares, axis=1, keepdims=True), axis=0, keepdims=True)
    root = jnp.sqrt(total * (1.0 / (COILS * 2 * SLABS * SLOTS * LANES)))
    rms[0] = root[0, 0]

    for copy in hops.values():
        copy.wait_send()
    for chunk in range(len(CHUNKS)):
        wait_all(send_a, len(CHUNKS[chunk]), PLANES, a_send.at[chunk])
    for group, (start, stop) in enumerate(GROUPS):
        wait_all(send_q, stop - start, KZ, b_send.at[group])
    for which, (buffer, size, *_) in enumerate(rounds):
        others = buffer.at[pl.ds(0, size - 1)]
        pltpu.make_async_copy(others, others, sum_send.at[which]).wait()


def per_device(image_est, coil_maps, kernel_tiles, tile_ids, tile_count, measured):
    hbm = pl.BlockSpec(memory_space=pl.ANY)
    vmem = pl.BlockSpec(memory_space=pltpu.VMEM)
    smem = pl.BlockSpec(memory_space=pltpu.SMEM)
    tables = [
        jnp.asarray(x_table()),
        jnp.asarray(long_table(0, 0)),
        jnp.asarray(y_table()),
        jnp.asarray(place_table()),
    ]
    residual, rms = pl.pallas_call(
        kernel,
        out_shape=(
            pltpu.VMEM((1, 2, SLOTS, LANES), F32),
            jax.ShapeDtypeStruct((1,), F32),
        ),
        in_specs=[hbm] * 10,
        out_specs=(vmem, smem),
        scratch_shapes=[
            pltpu.VMEM((8, 2, PLANES, YB, IMG), BF16),
            pltpu.VMEM((2, PLANES, IMG, IMG), BF16),
            pltpu.VMEM((SLOTS, LANES, 256), BF16),
            pltpu.SMEM((SLOTS,), jnp.int32),
            pltpu.SMEM((1,), jnp.int32),
            pltpu.VMEM((2, SLOTS, LANES), F32),
            pltpu.VMEM((2 * IMG, 2 * LANES), BF16),
            pltpu.VMEM((FREQ, 6 * IMG), BF16),
            pltpu.VMEM((FREQ, 4 * IMG), BF16),
            pltpu.VMEM((1024, 512), BF16),
            pltpu.VMEM((8, SLABS * PLANES, LANES), F32),
            pltpu.VMEM((8, SLABS * PLANES, LANES), F32),
            pltpu.VMEM((8, FREQ, LANES), F32),
            pltpu.VMEM((8, FREQ, LANES), F32),
            pltpu.VMEM((11, FREQ, LANES), jnp.int16),
            pltpu.VMEM((11, FREQ, LANES), jnp.int16),
            pltpu.VMEM((FREQ, LANES), F32),
            pltpu.VMEM((FREQ, LANES), F32),
            pltpu.VMEM((KZ * 64, 8, LANES), F32),
            pltpu.VMEM((SLOTS * 8, LANES), F32),
            pltpu.VMEM((2, SLOTS, 512), F32),
            pltpu.VMEM((COILS, 8, LANES), F32),
            pltpu.VMEM((SLABS, 8, LANES), F32),
            pltpu.SemaphoreType.DMA((10,)),
            pltpu.SemaphoreType.DMA((2, 4, 2)),
            pltpu.SemaphoreType.DMA((2, 4, 2)),
            pltpu.SemaphoreType.DMA((4,)),
            pltpu.SemaphoreType.DMA((4,)),
            pltpu.SemaphoreType.DMA((3,)),
            pltpu.SemaphoreType.DMA((3,)),
            pltpu.SemaphoreType.DMA((2,)),
            pltpu.SemaphoreType.DMA((2,)),
        ],
        compiler_params=pltpu.CompilerParams(
            collective_id=0, has_side_effects=True, vmem_limit_bytes=56 * 1024 * 1024
        ),
        cost_estimate=pl.CostEstimate(
            flops=6_000_000_000, bytes_accessed=20_000_000, transcendentals=0
        ),
    )(image_est, coil_maps, kernel_tiles, tile_ids, tile_count, measured, *tables)
    return residual, rms


def solution(mesh):
    placed = (
        P(None, "slab", "coil", None),
        P("coil", None, "slab", None, None),
        P("slab", None, None),
        P("slab"),
        P("slab"),
        P("coil", None, "slab", None),
    )
    return jax.shard_map(
        per_device,
        mesh=mesh,
        in_specs=placed,
        out_specs=(P("coil", None, "slab", None), P()),
        check_vma=False,
    )
```
